128 devices in a mesh: gx: 8 (over y, core), yz: 16 (over x, z).
Axes of the slice: x: 4, y: 4, z: 4, core: 2. Of those that a mesh axis runs over, the one named last changes fastest.
Arguments:
- composition: float32 [16384, 20, 128], P(('gx', 'yz')), may hold values from -6 to 6
- particle_mass: float32 [16384, 128], P(('gx', 'yz')), may hold values from 0.5 to 2
- mixing_rate: float32 [16384, 128], P(('gx', 'yz')), may hold values from 0.2 to 3
- cell_index: int32 [16384, 128], P(('gx', 'yz')), may hold values from 0 to 16383, as said below
- section_counts: int32 [16384], P(('gx', 'yz')), may hold values from 1 to 6, as said below
- block_shuffle: int32 [128, 128], P(('gx', 'yz')), may hold values from 0 to 127, as said below
- batch_inverse: float32 [128, 20, 20], P(('gx', 'yz')), may hold values from -1.25 to 1.25
- rate_exponents: float32 [84, 20], replicated, may hold values from -1.25 to 1.25
- stoichiometry: float32 [20, 84], replicated, may hold values from -0.625 to 0.625
Outputs:
- reacted: float32 [16384, 20, 128], P(('gx', 'yz'))
The draws below stay inside these ranges and needn't reach their ends.
Inputs may be any that keep to these rules, and one draw needn't show every extreme that they name: `cell_index`: A particle of the device at index i of gx and j of yz (d = i * 16 + j) lies in slab i - 1, i or i + 1, slab s holding cells s * 128 * 16 to (s + 1) * 128 * 16 - 1; that device's first 128 particles lie one each in cells d * 128 to d * 128 + 127. `section_counts`: some block has exactly 6 sections. `block_shuffle`: each row is a permutation of 0 to 127.
All inputs are finite; a program needn't handle non-finite values.
Results may differ from the reference program's by a relative error of at most 0.0011.
Values sent between devices are 32-bit elements; how exact they have to be, the bound alone decides.
A program may use at most 128 MiB of HBM per device.

```python
import math
import jax
import jax.numpy as jnp
from jax import lax

NS = 20
NR = 84
BLK = 128
SMAX = 6
BLOCKS_DEV = 128
CELL_DEV = 128
BLOCKS = 16384
CELLS = 16384
N_GX = 8
N_YZ = 16
DEVICES = 128


def draw_cell_index(key, part):
    per_device = BLOCKS_DEV * BLK
    slab_cells = CELL_DEV * N_YZ
    device = jnp.arange(DEVICES, dtype=jnp.int32)[:, None]
    slab_row = device // N_YZ
    first_key, second_key = jax.random.split(jax.random.fold_in(key, 11), 2)
    choose = jax.random.randint(first_key, (DEVICES, per_device), 0, 4)
    offset = jnp.where(choose == 0, -1, jnp.where(choose == 3, 1, 0))
    target = jnp.clip(slab_row + offset, 0, N_GX - 1)
    inside = jax.random.randint(second_key, (DEVICES, per_device), 0, slab_cells)
    placed = target * slab_cells + inside
    lane_index = jnp.arange(per_device, dtype=jnp.int32)[None, :]
    owned = device * CELL_DEV + lane_index
    placed = jnp.where(lane_index < CELL_DEV, owned, placed)
    return placed.reshape(BLOCKS, BLK).astype(jnp.int32)


def draw_section_counts(key, part):
    first_key, second_key, third_key = jax.random.split(jax.random.fold_in(key, 23), 3)
    level = jax.random.randint(first_key, (DEVICES, 1), 0, 3)
    ceiling = jnp.where(level == 0, 2, jnp.where(level == 1, 4, SMAX))
    drawn = jax.random.randint(second_key, (DEVICES, BLOCKS_DEV), 0, 1 << 20)
    counts = (1 + drawn % ceiling).reshape(-1)
    picked = jax.random.randint(third_key, (), 0, BLOCKS)
    counts = jnp.where(jnp.arange(BLOCKS) == picked, SMAX, counts)
    return counts.astype(jnp.int32)


def draw_block_shuffle(key, part):
    base = jnp.broadcast_to(jnp.arange(BLOCKS_DEV, dtype=jnp.int32), (DEVICES, BLOCKS_DEV))
    return jax.random.permutation(jax.random.fold_in(key, 37), base, axis=1, independent=True).astype(jnp.int32)


def levels(stream_key, extent, cuts, smallest, largest):
    loudness, own = 1.0, jax.random.fold_in(stream_key, 6)
    for axis_at, shards_of in cuts:
        steps = jnp.exp(jax.random.uniform(jax.random.fold_in(own, axis_at), (shards_of,), jnp.float32, smallest / len(cuts), largest / len(cuts)))
        loudness = loudness * jnp.repeat(steps, extent[axis_at] // shards_of).reshape([-1 if axis == axis_at else 1 for axis in range(len(extent))])
    return loudness


def scatter_about(key, extent, spread, bound, cuts=(), kind=jnp.bfloat16):
    array = jax.random.normal(key, extent, jnp.float32) * spread
    if len(cuts) > 0:
        array = levels(key, extent, cuts, -0.22, 0.18) * array
    return jnp.clip(array, min=-bound, max=bound).astype(kind)


def setup_inputs(seed: int = 0) -> dict:
    key_of = jax.random.split(jax.random.key(seed), 10)
    composition = scatter_about(key_of[0], (BLOCKS, NS, BLK), 1.0, 6.0, ((0, 128),), jnp.float32)
    particle_mass = jnp.clip(jnp.exp(math.log(2.0) - 1.3862944 * jax.random.uniform(key_of[1], (BLOCKS, BLK), jnp.float32) ** levels(key_of[1], (BLOCKS, BLK), ((0, 128),), -0.2, 0.2)), 0.5, 2.0)
    mixing_rate = jnp.clip(jnp.exp(math.log(3.0) - 2.7080502 * jax.random.uniform(key_of[2], (BLOCKS, BLK), jnp.float32) ** levels(key_of[2], (BLOCKS, BLK), ((0, 128),), -0.2, 0.2)), 0.2, 3.0)
    cell_index = draw_cell_index(jax.random.fold_in(key_of[9], 71), 0)
    section_counts = draw_section_counts(jax.random.fold_in(key_of[9], 71), 0)
    block_shuffle = draw_block_shuffle(jax.random.fold_in(key_of[9], 71), 0)
    batch_inverse = scatter_about(key_of[6], (DEVICES, NS, NS), NS ** -0.5, 1.25, ((0, 128),), jnp.float32)
    rate_exponents = scatter_about(key_of[7], (NR, NS), NS ** -0.5, 1.25, (), jnp.float32)
    stoichiometry = scatter_about(key_of[8], (NS, NR), NR ** -0.5, 0.625, (), jnp.float32)
    return {"composition": composition, "particle_mass": particle_mass, "mixing_rate": mixing_rate, "cell_index": cell_index, "section_counts": section_counts, "block_shuffle": block_shuffle, "batch_inverse": batch_inverse, "rate_exponents": rate_exponents, "stoichiometry": stoichiometry}


step_size = 0.25


def section_update(current, matrices, rate_exponents, stoichiometry):
    progress = jnp.tanh(jnp.einsum('rj,bjk->brk', rate_exponents, current, precision=lax.Precision.HIGHEST))
    forcing = jnp.einsum('ir,brk->bik', stoichiometry, progress, precision=lax.Precision.HIGHEST)
    return jnp.einsum('bij,bjk->bik', matrices, forcing, precision=lax.Precision.HIGHEST)


def reference(composition, particle_mass, mixing_rate, cell_index, section_counts, block_shuffle, batch_inverse, rate_exponents, stoichiometry):
    flat_cell = cell_index.reshape(-1)
    weighted = jnp.moveaxis(composition * particle_mass[:, None, :], 1, 0).reshape(NS, -1)
    cell_sum = jnp.zeros((NS, CELLS), jnp.float32).at[:, flat_cell].add(weighted)
    cell_mass = jnp.zeros((CELLS,), jnp.float32).at[flat_cell].add(particle_mass.reshape(-1))
    cell_means = cell_sum / cell_mass[None, :]
    looked = jnp.moveaxis(cell_means[:, flat_cell].reshape(NS, BLOCKS, BLK), 0, 1)
    mixed_state = looked + (composition - looked) * jnp.exp(-mixing_rate)[:, None, :]
    slot_of = jnp.argsort(block_shuffle, axis=1, stable=True)
    batch_of = (slot_of // (BLOCKS_DEV // DEVICES)).reshape(-1)
    group = 64
    groups = BLOCKS // group
    grouped_state = mixed_state.reshape(groups, group, NS, BLK)
    grouped_batch = batch_of.reshape(groups, group)
    grouped_counts = section_counts.reshape(groups, group)

    def one_group(inputs):
        current, batches, counts = inputs
        matrices = batch_inverse[batches]
        for section_index in range(SMAX):
            updated = current + step_size * section_update(current, matrices, rate_exponents, stoichiometry)
            current = jnp.where((counts > section_index)[:, None, None], updated, current)
        return current

    result = lax.map(one_group, (grouped_state, grouped_batch, grouped_counts))
    return result.reshape(BLOCKS, NS, BLK)
```

```python
import functools

import jax
import jax.numpy as jnp
from jax import lax
from jax.experimental import pallas as pl
from jax.experimental.pallas import tpu as pltpu
from jax.sharding import PartitionSpec as P

f32, bf16 = jnp.float32, jnp.bfloat16
MESH = pl.DeviceIdType.MESH
VMEM = pl.BlockSpec(memory_space=pltpu.VMEM)
SMEM = pl.BlockSpec(memory_space=pltpu.SMEM)

NS, NR, LANES = 20, 84, 128
CELL_DEV = 128
COLUMNS = 16
SLAB = CELL_DEV * COLUMNS
LOW = 256
HIGHS = 3 * SLAB // LOW
ROWS = 24
STEPS = 88
TILE = 8
GROUP = 8
STEP_SIZE = 0.25


def split(x):
    upper = x.astype(bf16)
    return upper, (x - upper.astype(f32)).astype(bf16)


def mm(a, b):
    return jnp.dot(a, b, preferred_element_type=f32)


def moments_kernel(
    comp_ref, mass_ref, cell_ref, counts_ref, shuffle_ref,
    part_ref, plan_ref, spread_ref, low_ref, acc_ref,
):
    blocks = comp_ref.shape[0]
    first = (lax.axis_index("gx") - 1) * SLAB
    iota = lax.broadcasted_iota(jnp.int32, (LOW, LANES), 0).astype(f32).astype(bf16)
    one, zero = jnp.ones((), bf16), jnp.zeros((), bf16)
    acc_ref[...] = jnp.zeros_like(acc_ref)

    def prepare(t, slot):
        base = pl.multiple_of(t * TILE, TILE)
        cells = cell_ref[pl.ds(base, TILE), :] - first
        high = (cells >> 8).astype(f32)
        low = (cells & (LOW - 1)).astype(f32)
        masses = mass_ref[pl.ds(base, TILE), :]
        for j in range(TILE):
            lanes = slice(j * LANES, (j + 1) * LANES)
            mass = masses[j : j + 1, :]
            value = jnp.concatenate(
                [comp_ref[base + j] * mass, mass, jnp.zeros((ROWS - NS - 1, LANES), f32)], 0
            )
            upper = value.astype(bf16).astype(f32)
            values = jnp.concatenate([upper, value - upper], 0).astype(bf16)
            high_row = jnp.broadcast_to(high[j : j + 1, :], (2 * ROWS, LANES)).astype(bf16)
            low_row = jnp.broadcast_to(low[j : j + 1, :], (LOW, LANES)).astype(bf16)
            for h in range(HIGHS):
                spread_ref[slot, h * 2 * ROWS : (h + 1) * 2 * ROWS, lanes] = jnp.where(
                    high_row == jnp.asarray(h, bf16), values, zero
                )
            low_ref[slot, :, lanes] = jnp.where(low_row == iota, one, zero)

    def multiply(slot):
        acc_ref[...] += lax.dot_general(
            spread_ref[slot], low_ref[slot], (((1,), (1,)), ((), ())), preferred_element_type=f32
        )

    def two_tiles(i, carry):
        prepare(2 * i, 0)
        multiply(0)
        prepare(2 * i + 1, 1)
        multiply(1)
        return carry

    lax.fori_loop(0, blocks // TILE // 2, two_tiles, 0)
    for h in range(HIGHS):
        total = acc_ref[h * 48 : h * 48 + 24, :] + acc_ref[h * 48 + 24 : h * 48 + 48, :]
        part_ref[2 * h] = total[:, :CELL_DEV]
        part_ref[2 * h + 1] = total[:, CELL_DEV:]

    row = lax.broadcasted_iota(jnp.int32, (blocks, blocks), 0)
    lane = lax.broadcasted_iota(jnp.int32, (blocks, blocks), 1)
    row_f, lane_f = row.astype(f32), lane.astype(f32)
    eye = row == lane
    counts = counts_ref[...].astype(f32)
    shuffle = shuffle_ref[...].astype(f32)
    block_of = jnp.sum(jnp.where(eye, shuffle, 0.0), axis=1, keepdims=True)
    count_of = jnp.sum(jnp.where(block_of == lane_f, counts, 0.0), axis=1, keepdims=True)
    count_row = jnp.sum(jnp.where(eye, count_of, 0.0), axis=0, keepdims=True)
    ahead = (count_row > count_of) | ((count_row == count_of) & (lane < row))
    rank = jnp.sum(jnp.where(ahead, 1.0, 0.0), axis=1, keepdims=True)
    here = rank == lane_f
    rows = [jnp.sum(jnp.where(here, v, 0.0), axis=0, keepdims=True) for v in (row_f, block_of, count_of)]
    plan_ref[...] = jnp.concatenate(rows + [jnp.zeros((5, blocks), f32)], 0).astype(jnp.int32)


def moments(composition, mass, cell, counts, shuffle):
    blocks = composition.shape[0]
    return pl.pallas_call(
        moments_kernel,
        out_shape=(
            jax.ShapeDtypeStruct((2 * HIGHS, ROWS, CELL_DEV), f32),
            jax.ShapeDtypeStruct((8, blocks), jnp.int32),
        ),
        in_specs=[VMEM] * 5,
        out_specs=(VMEM, VMEM),
        scratch_shapes=[
            pltpu.VMEM((2, HIGHS * 2 * ROWS, TILE * LANES), bf16),
            pltpu.VMEM((2, LOW, TILE * LANES), bf16),
            pltpu.VMEM((HIGHS * 2 * ROWS, LOW), f32),
        ],
        compiler_params=pltpu.CompilerParams(vmem_limit_bytes=50 << 20),
    )(composition, mass, cell, counts, shuffle)


def exchange_kernel(
    n_gx, part_ref, near_ref, halo_ref, own_ref, sums_ref, mine_ref,
    halo_send, halo_recv, sum_send, sum_recv, mean_send, mean_recv, slab_send, slab_recv,
):
    i, j = lax.axis_index("gx"), lax.axis_index("yz")
    left, right = lax.rem(i + n_gx - 1, n_gx), lax.rem(i + 1, n_gx)

    def column(p):
        return lax.rem(j + p, COLUMNS)

    def send(src, dst, send_sem, recv_sem, target):
        copy = pltpu.make_async_remote_copy(
            src_ref=src, dst_ref=dst, send_sem=send_sem, recv_sem=recv_sem,
            device_id=target, device_id_type=MESH,
        )
        copy.start()
        return copy

    barrier = pltpu.get_barrier_semaphore()
    for target in [(left, j), (right, j)] + [(i, column(p)) for p in range(1, COLUMNS)]:
        pl.semaphore_signal(barrier, inc=1, device_id=target, device_id_type=MESH)
    pl.semaphore_wait(barrier, COLUMNS + 1)

    def slab(s):
        return pl.ds(s * COLUMNS, COLUMNS)

    copies = [
        send(part_ref.at[slab(0)], halo_ref.at[1], halo_send.at[0], halo_recv.at[0], (left, j)),
        send(part_ref.at[slab(2)], halo_ref.at[0], halo_send.at[1], halo_recv.at[1], (right, j)),
    ]
    for copy in copies:
        copy.wait()
    own_ref[...] = part_ref[slab(1)] + halo_ref[0] + halo_ref[1]

    copies = [
        send(own_ref.at[column(p)], sums_ref.at[p], sum_send.at[p], sum_recv.at[p], (i, column(p)))
        for p in range(1, COLUMNS)
    ]
    total = own_ref[j]
    for p, copy in enumerate(copies, 1):
        copy.wait()
        total = total + sums_ref[p]
    means = total[:NS] / total[NS : NS + 1]
    mine_ref[...] = jnp.concatenate([means, jnp.zeros((ROWS - NS, CELL_DEV), f32)], 0)

    copies = [
        send(mine_ref, near_ref.at[COLUMNS + j], mean_send.at[p], mean_recv.at[p], (i, column(p)))
        for p in range(1, COLUMNS)
    ]
    near_ref[COLUMNS + j] = mine_ref[...]
    for copy in copies:
        copy.wait()

    copies = [
        send(near_ref.at[slab(1)], near_ref.at[slab(2)], slab_send.at[0], slab_recv.at[0], (left, j)),
        send(near_ref.at[slab(1)], near_ref.at[slab(0)], slab_send.at[1], slab_recv.at[1], (right, j)),
    ]
    for copy in copies:
        copy.wait()


def exchange(n_gx, part):
    dma = pltpu.SemaphoreType.DMA
    return pl.pallas_call(
        functools.partial(exchange_kernel, n_gx),
        out_shape=jax.ShapeDtypeStruct(part.shape, f32),
        in_specs=[VMEM],
        out_specs=VMEM,
        scratch_shapes=[
            pltpu.VMEM((2, COLUMNS, ROWS, CELL_DEV), f32),
            pltpu.VMEM((COLUMNS, ROWS, CELL_DEV), f32),
            pltpu.VMEM((COLUMNS, ROWS, CELL_DEV), f32),
            pltpu.VMEM((ROWS, CELL_DEV), f32),
            dma((2,)), dma((2,)), dma((COLUMNS,)), dma((COLUMNS,)),
            dma((COLUMNS,)), dma((COLUMNS,)), dma((2,)), dma((2,)),
        ],
        compiler_params=pltpu.CompilerParams(
            collective_id=0, has_side_effects=True, vmem_limit_bytes=20 << 20
        ),
    )(part)


def finish_kernel(
    plan_ref, comp_ref, rate_ref, cell_ref, near_ref, rates_ref, mats_ref,
    out_ref, state_ref, means_ref, low_ref, pick_ref, pair_ref,
):
    blocks = comp_ref.shape[0]
    first = (lax.axis_index("gx") - 1) * SLAB
    iota = lax.broadcasted_iota(jnp.int32, (LOW, LANES), 0).astype(f32).astype(bf16)
    one, zero = jnp.ones((), bf16), jnp.zeros((), bf16)
    for h in range(HIGHS):
        upper, lower = split(jnp.concatenate([near_ref[2 * h], near_ref[2 * h + 1]], 1))
        means_ref[h * ROWS : (h + 1) * ROWS, :LOW] = upper
        means_ref[h * ROWS : (h + 1) * ROWS, LOW:] = lower

    def prepare(t, slot):
        base = pl.multiple_of(t * TILE, TILE)
        low = ((cell_ref[pl.ds(base, TILE), :] - first) & (LOW - 1)).astype(f32)
        for j in range(TILE):
            lanes = slice(j * LANES, (j + 1) * LANES)
            low_row = jnp.broadcast_to(low[j : j + 1, :], (LOW, LANES)).astype(bf16)
            table = jnp.where(low_row == iota, one, zero)
            low_ref[slot, :LOW, lanes] = table
            low_ref[slot, LOW:, lanes] = table

    def multiply(slot):
        pick_ref[slot] = mm(means_ref[...], low_ref[slot])

    def mix(t, slot):
        base = pl.multiple_of(t * TILE, TILE)
        high = (cell_ref[pl.ds(base, TILE), :] - first) >> 8
        decay = jnp.exp(-rate_ref[pl.ds(base, TILE), :])
        for j in range(TILE):
            lanes = slice(j * LANES, (j + 1) * LANES)
            high_row = jnp.broadcast_to(high[j : j + 1, :], (ROWS, LANES))
            mean = jnp.zeros((ROWS, LANES), f32)
            for h in range(HIGHS):
                mean = jnp.where(high_row == h, pick_ref[slot, h * ROWS : (h + 1) * ROWS, lanes], mean)
            mean = mean[:NS]
            state_ref[base + j, :NS] = mean + (comp_ref[base + j] - mean) * decay[j : j + 1, :]
            state_ref[base + j, NS:] = jnp.zeros((ROWS - NS, LANES), f32)

    def two_tiles(i, carry):
        prepare(2 * i, 0)
        multiply(0)
        mix(2 * i, 0)
        prepare(2 * i + 1, 1)
        multiply(1)
        mix(2 * i + 1, 1)
        return carry

    lax.fori_loop(0, blocks // TILE // 2, two_tiles, 0)
    rates = rates_ref[...]

    def group(g, carry):
        at = [g * GROUP + b for b in range(GROUP)]
        block = [plan_ref[1, a] for a in at]
        need = [plan_ref[2, a] for a in at]
        for b in range(GROUP):
            upper, lower = split(mats_ref[plan_ref[0, at[b]]])
            pair_ref[b] = jnp.concatenate([upper.astype(f32), lower.astype(f32)], 0).astype(bf16)
        pairs = [pair_ref[b][:, :STEPS] for b in range(GROUP)]

        def section(s, states):
            after = []
            for b in range(0, GROUP, 2):
                x = jnp.concatenate(states[b : b + 2], 1)
                upper = x.astype(bf16).astype(f32)
                parts = jnp.concatenate([upper, x - upper, upper], 0).astype(bf16)
                t_upper, t_lower = split(jnp.tanh(mm(rates, parts)))
                y = mm(jnp.concatenate(pairs[b : b + 2], 0), t_upper)
                z = mm(jnp.concatenate([pairs[b][:ROWS], pairs[b + 1][:ROWS]], 0), t_lower)
                first_change = y[:24, :LANES] + y[24:48, :LANES] + z[:24, :LANES]
                second_change = y[48:72, LANES:] + y[72:, LANES:] + z[24:, LANES:]
                after.append(jnp.where(s < need[b], states[b] + first_change, states[b]))
                after.append(jnp.where(s < need[b + 1], states[b + 1] + second_change, states[b + 1]))
            return tuple(after)

        states = lax.fori_loop(0, need[0], section, tuple(state_ref[b] for b in block))
        for b in range(GROUP):
            out_ref[block[b]] = states[b][:NS]
        return carry

    lax.fori_loop(0, blocks // GROUP, group, 0)


def finish(plan, composition, rate, cell, near, rates, mats):
    return pl.pallas_call(
        finish_kernel,
        out_shape=jax.ShapeDtypeStruct(composition.shape, f32),
        in_specs=[SMEM] + [VMEM] * 6,
        out_specs=VMEM,
        scratch_shapes=[
            pltpu.VMEM((composition.shape[0], ROWS, LANES), f32),
            pltpu.VMEM((HIGHS * ROWS, 2 * LOW), bf16),
            pltpu.VMEM((2, 2 * LOW, TILE * LANES), bf16),
            pltpu.VMEM((2, HIGHS * ROWS, TILE * LANES), f32),
            pltpu.VMEM((GROUP, 2 * ROWS, LANES), bf16),
        ],
        compiler_params=pltpu.CompilerParams(vmem_limit_bytes=50 << 20),
    )(plan, composition, rate, cell, near, rates, mats)


def local(
    n_gx, composition, particle_mass, mixing_rate, cell_index, section_counts,
    block_shuffle, batch_inverse, rate_exponents, stoichiometry,
):
    mat = STEP_SIZE * jnp.dot(batch_inverse[0], stoichiometry, precision=lax.Precision.HIGHEST)
    mat = jnp.pad(mat, ((0, ROWS - NS), (0, LANES - NR)))
    mats = lax.all_gather(mat, ("gx", "yz"), axis=0)
    rates = jnp.pad(rate_exponents, ((0, STEPS - NR), (0, ROWS - NS)))
    upper = lax.reduce_precision(rates, 8, 7)
    rates = jnp.concatenate([upper, upper, rates - upper], 1).astype(bf16)
    part, plan = moments(composition, particle_mass, cell_index, section_counts[None], block_shuffle)
    near = exchange(n_gx, part)
    return finish(plan, composition, mixing_rate, cell_index, near, rates, mats)


def solution(mesh):
    both = ("gx", "yz")
    in_specs = (
        P(both, None, None), P(both, None), P(both, None), P(both, None), P(both),
        P(both, None), P(both, None, None), P(), P(),
    )
    return jax.shard_map(
        functools.partial(local, mesh.shape["gx"]),
        mesh=mesh, in_specs=in_specs, out_specs=P(both, None, None), check_vma=False,
    )
```

```python
import functools

import jax
import jax.numpy as jnp
from jax import lax
from jax.experimental import pallas as pl
from jax.experimental.pallas import tpu as pltpu
from jax.sharding import PartitionSpec as P

f32, bf16 = jnp.float32, jnp.bfloat16
MESH = pl.DeviceIdType.MESH
VMEM = pl.BlockSpec(memory_space=pltpu.VMEM)
SMEM = pl.BlockSpec(memory_space=pltpu.SMEM)

NS, NR, LANES = 20, 84, 128
CELL_DEV = 128
COLUMNS = 16
SLAB = CELL_DEV * COLUMNS
LOW = 256
HIGHS = 3 * SLAB // LOW
ROWS = 24
STEPS = 88
TILE = 8
GROUP = 32
STEP_SIZE = 0.25
PACK = 4


def split(x):
    upper = x.astype(bf16)
    return upper, (x - upper.astype(f32)).astype(bf16)


def mm(a, b):
    return jnp.dot(a, b, preferred_element_type=f32)


def moments_kernel(
    comp_ref, mass_ref, cell_ref, counts_ref, shuffle_ref,
    part_ref, plan_ref, spread_ref, low_ref, acc_ref,
):
    blocks = comp_ref.shape[0]
    first = (lax.axis_index("gx") - 1) * SLAB
    iota = lax.broadcasted_iota(jnp.int32, (LOW, LANES), 0).astype(f32).astype(bf16)
    one, zero = jnp.ones((), bf16), jnp.zeros((), bf16)
    acc_ref[...] = jnp.zeros_like(acc_ref)

    def prepare(t, slot):
        base = pl.multiple_of(t * TILE, TILE)
        cells = cell_ref[pl.ds(base, TILE), :] - first
        high = (cells >> 8).astype(f32)
        low = (cells & (LOW - 1)).astype(f32)
        masses = mass_ref[pl.ds(base, TILE), :]
        for j in range(TILE):
            lanes = slice(j * LANES, (j + 1) * LANES)
            mass = masses[j : j + 1, :]
            value = jnp.concatenate(
                [comp_ref[base + j] * mass, mass, jnp.zeros((ROWS - NS - 1, LANES), f32)], 0
            )
            upper = value.astype(bf16).astype(f32)
            values = jnp.concatenate([upper, value - upper], 0).astype(bf16)
            high_row = jnp.broadcast_to(high[j : j + 1, :], (2 * ROWS, LANES)).astype(bf16)
            low_row = jnp.broadcast_to(low[j : j + 1, :], (LOW, LANES)).astype(bf16)
            for h in range(HIGHS):
                spread_ref[slot, h * 2 * ROWS : (h + 1) * 2 * ROWS, lanes] = jnp.where(
                    high_row == jnp.asarray(h, bf16), values, zero
                )
            low_ref[slot, :, lanes] = jnp.where(low_row == iota, one, zero)

    def multiply(slot):
        acc_ref[...] += lax.dot_general(
            spread_ref[slot], low_ref[slot], (((1,), (1,)), ((), ())), preferred_element_type=f32
        )

    def two_tiles(i, carry):
        prepare(2 * i, 0)
        multiply(0)
        prepare(2 * i + 1, 1)
        multiply(1)
        return carry

    lax.fori_loop(0, blocks // TILE // 2, two_tiles, 0)
    for h in range(HIGHS):
        total = acc_ref[h * 48 : h * 48 + 24, :] + acc_ref[h * 48 + 24 : h * 48 + 48, :]
        part_ref[2 * h] = total[:, :CELL_DEV]
        part_ref[2 * h + 1] = total[:, CELL_DEV:]

    row = lax.broadcasted_iota(jnp.int32, (blocks, blocks), 0)
    lane = lax.broadcasted_iota(jnp.int32, (blocks, blocks), 1)
    lane_f = lane.astype(f32)
    place = ((row % COLUMNS) * (blocks // COLUMNS) + row // COLUMNS).astype(f32)
    eye = row == lane
    counts = counts_ref[...].astype(f32)
    shuffle = shuffle_ref[...].astype(f32)
    block_of = jnp.sum(jnp.where(eye, shuffle, 0.0), axis=1, keepdims=True)
    count_of = jnp.sum(jnp.where(block_of == lane_f, counts, 0.0), axis=1, keepdims=True)
    count_row = jnp.sum(jnp.where(eye, count_of, 0.0), axis=0, keepdims=True)
    ahead = (count_row > count_of) | ((count_row == count_of) & (lane < row))
    rank = jnp.sum(jnp.where(ahead, 1.0, 0.0), axis=1, keepdims=True)
    here = rank == lane_f
    rows = [jnp.sum(jnp.where(here, v, 0.0), axis=0, keepdims=True) for v in (place, block_of, count_of)]
    plan_ref[...] = jnp.concatenate(rows + [jnp.zeros((5, blocks), f32)], 0).astype(jnp.int32)


def moments(composition, mass, cell, counts, shuffle):
    blocks = composition.shape[0]
    return pl.pallas_call(
        moments_kernel,
        out_shape=(
            jax.ShapeDtypeStruct((2 * HIGHS, ROWS, CELL_DEV), f32),
            jax.ShapeDtypeStruct((8, blocks), jnp.int32),
        ),
        in_specs=[VMEM] * 5,
        out_specs=(VMEM, VMEM),
        scratch_shapes=[
            pltpu.VMEM((2, HIGHS * 2 * ROWS, TILE * LANES), bf16),
            pltpu.VMEM((2, LOW, TILE * LANES), bf16),
            pltpu.VMEM((HIGHS * 2 * ROWS, LOW), f32),
        ],
        compiler_params=pltpu.CompilerParams(vmem_limit_bytes=50 << 20),
    )(composition, mass, cell, counts, shuffle)


def exchange_kernel(
    n_gx, part_ref, packed_ref, stoich_ref, near_ref, mats_ref,
    halo_ref, own_ref, sums_ref, mine_ref, batch_ref, wide_ref,
    halo_send, halo_recv, sum_send, sum_recv, mean_send, mean_recv, slab_send, slab_recv,
    row_send, row_recv, batch_send, batch_recv,
):
    i, j = lax.axis_index("gx"), lax.axis_index("yz")
    left, right = lax.rem(i + n_gx - 1, n_gx), lax.rem(i + 1, n_gx)

    def column(p):
        return lax.rem(j + p, COLUMNS)

    def gx_peer(p):
        return lax.rem(i + p, n_gx)

    def send(src, dst, send_sem, recv_sem, target):
        copy = pltpu.make_async_remote_copy(
            src_ref=src, dst_ref=dst, send_sem=send_sem, recv_sem=recv_sem,
            device_id=target, device_id_type=MESH,
        )
        copy.start()
        return copy

    def slab(s):
        return pl.ds(s * COLUMNS, COLUMNS)

    barrier = pltpu.get_barrier_semaphore()
    peers = [(gx_peer(p), j) for p in range(1, n_gx)] + [(i, column(p)) for p in range(1, COLUMNS)]
    for target in peers:
        pl.semaphore_signal(barrier, inc=1, device_id=target, device_id_type=MESH)
    batch_ref[j, i] = packed_ref[...]
    pl.semaphore_wait(barrier, len(peers))

    halos = [
        send(part_ref.at[slab(0)], halo_ref.at[1], halo_send.at[0], halo_recv.at[0], (left, j)),
        send(part_ref.at[slab(2)], halo_ref.at[0], halo_send.at[1], halo_recv.at[1], (right, j)),
    ]
    rows = [
        send(batch_ref.at[j, i], batch_ref.at[j, i], row_send.at[p], row_recv.at[p], (gx_peer(p), j))
        for p in range(1, n_gx)
    ]
    for copy in halos:
        copy.wait()
    own_ref[...] = part_ref[slab(1)] + halo_ref[0] + halo_ref[1]

    partials = [
        send(own_ref.at[column(p)], sums_ref.at[p], sum_send.at[p], sum_recv.at[p], (i, column(p)))
        for p in range(1, COLUMNS)
    ]
    for copy in rows:
        copy.wait()
    batches = [
        send(batch_ref.at[j], batch_ref.at[j], batch_send.at[p], batch_recv.at[p], (i, column(p)))
        for p in range(1, COLUMNS)
    ]
    wide_ref[...] = jnp.zeros_like(wide_ref)
    upper, lower = (v.astype(f32) for v in split(STEP_SIZE * stoich_ref[...]))
    for c in range(NS // PACK):
        lanes = slice(c * LANES, c * LANES + NR)
        for k, piece in enumerate((upper, lower, upper)):
            wide_ref[k * LANES + c * ROWS : k * LANES + c * ROWS + NS, lanes] = piece

    total = own_ref[j]
    for p, copy in enumerate(partials, 1):
        copy.wait()
        total = total + sums_ref[p]
    means = total[:NS] / total[NS : NS + 1]
    mine_ref[...] = jnp.concatenate([means, jnp.zeros((ROWS - NS, CELL_DEV), f32)], 0)

    copies = [
        send(mine_ref, near_ref.at[COLUMNS + j], mean_send.at[p], mean_recv.at[p], (i, column(p)))
        for p in range(1, COLUMNS)
    ]
    near_ref[COLUMNS + j] = mine_ref[...]
    for copy in copies:
        copy.wait()

    slabs = [
        send(near_ref.at[slab(1)], near_ref.at[slab(2)], slab_send.at[0], slab_recv.at[0], (left, j)),
        send(near_ref.at[slab(1)], near_ref.at[slab(0)], slab_send.at[1], slab_recv.at[1], (right, j)),
    ]

    for copy in batches:
        copy.wait()
    wide = wide_ref[...].astype(bf16)
    batch_total = n_gx * COLUMNS
    for t in range(PACK):
        upper, lower = split(batch_ref[:, :, t, :].reshape(batch_total, LANES))
        product = mm(jnp.concatenate([upper, upper, lower], 1), wide)
        for c in range(NS // PACK):
            mats_ref[:, PACK * c + t, :] = product[:, c * LANES : (c + 1) * LANES]
    for r in range(NS, ROWS):
        mats_ref[:, r, :] = jnp.zeros((batch_total, LANES), f32)
    for copy in slabs:
        copy.wait()


def exchange(n_gx, part, packed, stoichiometry):
    dma = pltpu.SemaphoreType.DMA
    return pl.pallas_call(
        functools.partial(exchange_kernel, n_gx),
        out_shape=(
            jax.ShapeDtypeStruct(part.shape, f32),
            jax.ShapeDtypeStruct((n_gx * COLUMNS, ROWS, LANES), f32),
        ),
        in_specs=[VMEM] * 3,
        out_specs=(VMEM, VMEM),
        scratch_shapes=[
            pltpu.VMEM((2, COLUMNS, ROWS, CELL_DEV), f32),
            pltpu.VMEM((COLUMNS, ROWS, CELL_DEV), f32),
            pltpu.VMEM((COLUMNS, ROWS, CELL_DEV), f32),
            pltpu.VMEM((ROWS, CELL_DEV), f32),
            pltpu.VMEM((COLUMNS, n_gx, PACK, LANES), f32),
            pltpu.VMEM((3 * LANES, NS // PACK * LANES), f32),
            dma((2,)), dma((2,)), dma((COLUMNS,)), dma((COLUMNS,)),
            dma((COLUMNS,)), dma((COLUMNS,)), dma((2,)), dma((2,)),
            dma((n_gx,)), dma((n_gx,)), dma((COLUMNS,)), dma((COLUMNS,)),
        ],
        compiler_params=pltpu.CompilerParams(
            collective_id=0, has_side_effects=True, vmem_limit_bytes=20 << 20
        ),
    )(part, packed, stoichiometry)


def finish_kernel(
    plan_ref, comp_ref, rate_ref, cell_ref, near_ref, rates_ref, mats_ref,
    out_ref, state_ref, means_ref, low_ref, pick_ref, pair_ref, turn_ref,
):
    blocks = comp_ref.shape[0]
    first = (lax.axis_index("gx") - 1) * SLAB
    iota = lax.broadcasted_iota(jnp.int32, (LOW, LANES), 0).astype(f32).astype(bf16)
    one, zero = jnp.ones((), bf16), jnp.zeros((), bf16)
    for h in range(HIGHS):
        upper, lower = split(jnp.concatenate([near_ref[2 * h], near_ref[2 * h + 1]], 1))
        means_ref[h * ROWS : (h + 1) * ROWS, :LOW] = upper
        means_ref[h * ROWS : (h + 1) * ROWS, LOW:] = lower

    def prepare(t, slot):
        base = pl.multiple_of(t * TILE, TILE)
        low = ((cell_ref[pl.ds(base, TILE), :] - first) & (LOW - 1)).astype(f32)
        for j in range(TILE):
            lanes = slice(j * LANES, (j + 1) * LANES)
            low_row = jnp.broadcast_to(low[j : j + 1, :], (LOW, LANES)).astype(bf16)
            table = jnp.where(low_row == iota, one, zero)
            low_ref[slot, :LOW, lanes] = table
            low_ref[slot, LOW:, lanes] = table

    def multiply(slot):
        pick_ref[slot] = mm(means_ref[...], low_ref[slot])

    def mix(t, slot):
        base = pl.multiple_of(t * TILE, TILE)
        high = (cell_ref[pl.ds(base, TILE), :] - first) >> 8
        decay = jnp.exp(-rate_ref[pl.ds(base, TILE), :])
        for j in range(TILE):
            lanes = slice(j * LANES, (j + 1) * LANES)
            high_row = jnp.broadcast_to(high[j : j + 1, :], (ROWS, LANES))
            mean = jnp.zeros((ROWS, LANES), f32)
            for h in range(HIGHS):
                mean = jnp.where(high_row == h, pick_ref[slot, h * ROWS : (h + 1) * ROWS, lanes], mean)
            mean = mean[:NS]
            state_ref[base + j, :NS] = mean + (comp_ref[base + j] - mean) * decay[j : j + 1, :]
            state_ref[base + j, NS:] = jnp.zeros((ROWS - NS, LANES), f32)

    def two_tiles(i, carry):
        prepare(2 * i, 0)
        multiply(0)
        mix(2 * i, 0)
        prepare(2 * i + 1, 1)
        multiply(1)
        mix(2 * i + 1, 1)
        return carry

    lax.fori_loop(0, blocks // TILE // 2, two_tiles, 0)
    turn_ref[...] = jnp.zeros_like(turn_ref)
    upper, lower = (v.astype(f32) for v in split(rates_ref[...]))
    for k, piece in enumerate((upper, upper, lower)):
        turn_ref[k * ROWS : k * ROWS + NS, :NR] = piece
    rates = turn_ref[...].T[:STEPS, : 3 * ROWS].astype(bf16)
    lane = lax.broadcasted_iota(jnp.int32, (ROWS, LANES), 1)

    def group(g, carry):
        at = [g * GROUP + b for b in range(GROUP)]
        block = [plan_ref[1, a] for a in at]
        need = [plan_ref[2, a] for a in at]
        for b in range(GROUP):
            upper, lower = (v.astype(f32) for v in split(mats_ref[plan_ref[0, at[b]]]))
            turned = pltpu.roll(upper, STEPS, 1)
            head = jnp.where(lane < STEPS, upper, turned)
            tail = jnp.where(lane < 2 * STEPS - LANES, turned, 0.0)
            pair_ref[b, :, :LANES] = jnp.concatenate([head, lower], 0).astype(bf16)
            pair_ref[b, :, LANES:] = jnp.concatenate([tail, jnp.zeros((ROWS, LANES), f32)], 0).astype(bf16)

        def section(s, states):
            x = jnp.concatenate(states, 1)
            upper = x.astype(bf16).astype(f32)
            progress = jnp.tanh(mm(rates, jnp.concatenate([upper, x - upper, upper], 0).astype(bf16)))
            upper = progress.astype(bf16).astype(f32)
            progress = jnp.concatenate([upper, progress - upper], 0).astype(bf16)
            products = [
                mm(
                    pair_ref[b : b + 2].reshape(4 * ROWS, 2 * LANES)[:, : 2 * STEPS],
                    progress[:, b * LANES : (b + 2) * LANES],
                )
                for b in range(0, GROUP, 2)
            ]
            after = []
            for b, y in zip(range(0, GROUP, 2), products):
                first_change = y[:24, :LANES] + y[24:48, :LANES]
                second_change = y[48:72, LANES:] + y[72:, LANES:]
                after.append(jnp.where(s < need[b], states[b] + first_change, states[b]))
                after.append(jnp.where(s < need[b + 1], states[b + 1] + second_change, states[b + 1]))
            return tuple(after)

        states = lax.fori_loop(0, need[0], section, tuple(state_ref[b] for b in block))
        for b in range(GROUP):
            out_ref[block[b]] = states[b][:NS]
        return carry

    lax.fori_loop(0, blocks // GROUP, group, 0)


def finish(plan, composition, rate, cell, near, rates, mats):
    return pl.pallas_call(
        finish_kernel,
        out_shape=jax.ShapeDtypeStruct(composition.shape, f32),
        in_specs=[SMEM] + [VMEM] * 6,
        out_specs=VMEM,
        scratch_shapes=[
            pltpu.VMEM((composition.shape[0], ROWS, LANES), f32),
            pltpu.VMEM((HIGHS * ROWS, 2 * LOW), bf16),
            pltpu.VMEM((2, 2 * LOW, TILE * LANES), bf16),
            pltpu.VMEM((2, HIGHS * ROWS, TILE * LANES), f32),
            pltpu.VMEM((GROUP, 2 * ROWS, 2 * LANES), bf16),
            pltpu.VMEM((LANES, LANES), f32),
        ],
        compiler_params=pltpu.CompilerParams(vmem_limit_bytes=50 << 20),
    )(plan, composition, rate, cell, near, rates, mats)


def local(
    n_gx, composition, particle_mass, mixing_rate, cell_index, section_counts,
    block_shuffle, batch_inverse, rate_exponents, stoichiometry,
):
    part, plan = moments(composition, particle_mass, cell_index, section_counts[None], block_shuffle)
    packed = jnp.pad(batch_inverse[0], ((0, 0), (0, ROWS - NS)))
    packed = packed.reshape(NS // PACK, PACK, ROWS).transpose(1, 0, 2).reshape(PACK, NS // PACK * ROWS)
    packed = jnp.pad(packed, ((0, 0), (0, LANES - NS // PACK * ROWS)))
    near, mats = exchange(n_gx, part, packed, stoichiometry)
    return finish(plan, composition, mixing_rate, cell_index, near, rate_exponents.T, mats)


def solution(mesh):
    both = ("gx", "yz")
    in_specs = (
        P(both, None, None), P(both, None), P(both, None), P(both, None), P(both),
        P(both, None), P(both, None, None), P(), P(),
    )
    return jax.shard_map(
        functools.partial(local, mesh.shape["gx"]),
        mesh=mesh, in_specs=in_specs, out_specs=P(both, None, None), check_vma=False,
    )
```

```python
import functools

import jax
import jax.numpy as jnp
from jax import lax
from jax.experimental import pallas as pl
from jax.experimental.pallas import tpu as pltpu
from jax.sharding import PartitionSpec as P

f32, bf16 = jnp.float32, jnp.bfloat16
MESH = pl.DeviceIdType.MESH
VMEM = pl.BlockSpec(memory_space=pltpu.VMEM)
SMEM = pl.BlockSpec(memory_space=pltpu.SMEM)

NS, NR, LANES = 20, 84, 128
CELL_DEV = 128
COLUMNS = 16
SLAB = CELL_DEV * COLUMNS
LOW = 256
HIGHS = 3 * SLAB // LOW
ROWS = 24
STEPS = 88
TILE = 8
GROUP = 32
STEP_SIZE = 0.25
PACK = 4


def split(x):
    upper = x.astype(bf16)
    return upper, (x - upper.astype(f32)).astype(bf16)


def mm(a, b):
    return jnp.dot(a, b, preferred_element_type=f32)


def gather_kernel(
    n_gx, comp_ref, mass_ref, rate_ref, cell_ref, counts_ref, shuffle_ref, packed_ref, stoich_ref,
    state_ref, mats_ref, plan_ref,
    value_ref, low_ref, spread_ref, acc_ref, pick_ref, table_ref, part_ref, halo_ref, own_ref, sums_ref,
    mine_ref, near_ref, batch_ref, wide_ref,
    halo_send, halo_recv, sum_send, sum_recv, mean_send, mean_recv, left_send, left_recv,
    right_send, right_recv, row_send, row_recv, batch_send, batch_recv,
):
    blocks = mass_ref.shape[0]
    tiles = blocks // TILE
    i, j = lax.axis_index("gx"), lax.axis_index("yz")
    left, right = lax.rem(i + n_gx - 1, n_gx), lax.rem(i + 1, n_gx)
    first = (i - 1) * SLAB
    iota = lax.broadcasted_iota(jnp.int32, (LOW, LANES), 0).astype(f32).astype(bf16)
    one, zero = jnp.ones((), bf16), jnp.zeros((), bf16)
    own_highs = range(HIGHS // 3, 2 * HIGHS // 3)
    other_highs = [h for h in range(HIGHS) if h not in own_highs]

    def column(p):
        return lax.rem(j + p, COLUMNS)

    def gx_peer(p):
        return lax.rem(i + p, n_gx)

    def send(src, dst, send_sem, recv_sem, target):
        copy = pltpu.make_async_remote_copy(
            src_ref=src, dst_ref=dst, send_sem=send_sem, recv_sem=recv_sem,
            device_id=target, device_id_type=MESH,
        )
        copy.start()
        return copy

    barrier = pltpu.get_barrier_semaphore()
    peers = [(gx_peer(p), j) for p in range(1, n_gx)] + [(i, column(p)) for p in range(1, COLUMNS)]
    for target in peers:
        pl.semaphore_signal(barrier, inc=1, device_id=target, device_id_type=MESH)
    batch_ref[j, i] = packed_ref[...]

    def prepare(t):
        base = pl.multiple_of(t * TILE, TILE)
        low = ((cell_ref[pl.ds(base, TILE), :] - first) & (LOW - 1)).astype(f32)
        masses = mass_ref[pl.ds(base, TILE), :]
        for b in range(TILE):
            lanes = slice(b * LANES, (b + 1) * LANES)
            mass = masses[b : b + 1, :]
            value = jnp.concatenate(
                [comp_ref[:, base + b, :] * mass, mass, jnp.zeros((ROWS - NS - 1, LANES), f32)], 0
            )
            upper = value.astype(bf16).astype(f32)
            value_ref[t, :, lanes] = jnp.concatenate([upper, value - upper], 0).astype(bf16)
            low_row = jnp.broadcast_to(low[b : b + 1, :], (LOW, LANES)).astype(bf16)
            low_ref[t, :, lanes] = jnp.where(low_row == iota, one, zero)

    def spread(t, slot, highs):
        base = pl.multiple_of(t * TILE, TILE)
        high = ((cell_ref[pl.ds(base, TILE), :] - first) >> 8).astype(f32)
        for b in range(TILE):
            lanes = slice(b * LANES, (b + 1) * LANES)
            values = value_ref[t, :, lanes]
            high_row = jnp.broadcast_to(high[b : b + 1, :], (2 * ROWS, LANES)).astype(bf16)
            for k, h in enumerate(highs):
                spread_ref[slot, k * 2 * ROWS : (k + 1) * 2 * ROWS, lanes] = jnp.where(
                    high_row == jnp.asarray(h, bf16), values, zero
                )

    def accumulate(t, slot, highs):
        rows = len(highs) * 2 * ROWS
        acc_ref[:rows] += lax.dot_general(
            spread_ref[slot, :rows], low_ref[t], (((1,), (1,)), ((), ())), preferred_element_type=f32
        )

    def owners(highs):
        for k, h in enumerate(highs):
            total = acc_ref[k * 48 : k * 48 + 24, :] + acc_ref[k * 48 + 24 : k * 48 + 48, :]
            yield k, total[:, :CELL_DEV], total[:, CELL_DEV:]

    acc_ref[...] = jnp.zeros_like(acc_ref)

    def other_tiles(u, carry):
        for slot in range(2):
            prepare(2 * u + slot)
            spread(2 * u + slot, slot, other_highs)
            accumulate(2 * u + slot, slot, other_highs)
        return carry

    lax.fori_loop(0, tiles // 2, other_tiles, 0)
    for k, even, odd in owners(other_highs):
        part_ref[2 * k] = even
        part_ref[2 * k + 1] = odd
    acc_ref[...] = jnp.zeros_like(acc_ref)

    pl.semaphore_wait(barrier, len(peers))
    halos = [
        send(part_ref.at[pl.ds(0, COLUMNS)], halo_ref.at[1], halo_send.at[0], halo_recv.at[0], (left, j)),
        send(part_ref.at[pl.ds(COLUMNS, COLUMNS)], halo_ref.at[0], halo_send.at[1], halo_recv.at[1], (right, j)),
    ]
    rows = [
        send(batch_ref.at[j, i], batch_ref.at[j, i], row_send.at[p], row_recv.at[p], (gx_peer(p), j))
        for p in range(1, n_gx)
    ]

    def own_tiles(u, carry):
        for slot in range(2):
            spread(2 * u + slot, slot, own_highs)
            accumulate(2 * u + slot, slot, own_highs)
        return carry

    lax.fori_loop(0, tiles // 4, own_tiles, 0)
    for copy in rows:
        copy.wait()
    batches = [
        send(batch_ref.at[j], batch_ref.at[j], batch_send.at[p], batch_recv.at[p], (i, column(p)))
        for p in range(1, COLUMNS)
    ]
    lax.fori_loop(tiles // 4, tiles // 2, own_tiles, 0)
    for copy in halos:
        copy.wait()
    for k, even, odd in owners(own_highs):
        own_ref[2 * k] = even + halo_ref[0, 2 * k] + halo_ref[1, 2 * k]
        own_ref[2 * k + 1] = odd + halo_ref[0, 2 * k + 1] + halo_ref[1, 2 * k + 1]

    partials = [
        send(own_ref.at[column(p)], sums_ref.at[p], sum_send.at[p], sum_recv.at[p], (i, column(p)))
        for p in range(1, COLUMNS)
    ]

    wide_ref[...] = jnp.zeros_like(wide_ref)
    upper, lower = (v.astype(f32) for v in split(STEP_SIZE * stoich_ref[...]))
    for c in range(NS // PACK):
        lanes = slice(c * LANES, c * LANES + NR)
        for k, piece in enumerate((upper, lower, upper)):
            wide_ref[k * LANES + c * ROWS : k * LANES + c * ROWS + NS, lanes] = piece
    wide = wide_ref[...].astype(bf16)
    for copy in batches:
        copy.wait()
    batch_total = n_gx * COLUMNS
    for t in range(PACK):
        upper, lower = split(batch_ref[:, :, t, :].reshape(batch_total, LANES))
        product = mm(jnp.concatenate([upper, upper, lower], 1), wide)
        for c in range(NS // PACK):
            mats_ref[:, PACK * c + t, :] = product[:, c * LANES : (c + 1) * LANES]
    for r in range(NS, ROWS):
        mats_ref[:, r, :] = jnp.zeros((batch_total, LANES), f32)

    total = own_ref[j]
    for p, copy in enumerate(partials, 1):
        copy.wait()
        total = total + sums_ref[p]
    means = total[:NS] / total[NS : NS + 1]
    mine_ref[...] = jnp.concatenate([means, jnp.zeros((ROWS - NS, CELL_DEV), f32)], 0)

    slab_means = [
        send(mine_ref, near_ref.at[COLUMNS + j], mean_send.at[p], mean_recv.at[p], (i, column(p)))
        for p in range(1, COLUMNS)
    ]
    near_ref[COLUMNS + j] = mine_ref[...]

    def forward(p, src, at):
        return [
            send(src, near_ref.at[2 * COLUMNS + at], left_send.at[p], left_recv.at[p], (left, j)),
            send(src, near_ref.at[at], right_send.at[p], right_recv.at[p], (right, j)),
        ]

    forwards = forward(0, mine_ref, j)

    row = lax.broadcasted_iota(jnp.int32, (blocks, blocks), 0)
    lane = lax.broadcasted_iota(jnp.int32, (blocks, blocks), 1)
    lane_f = lane.astype(f32)
    place = ((row % COLUMNS) * (blocks // COLUMNS) + row // COLUMNS).astype(f32)
    eye = row == lane
    counts = counts_ref[...].astype(f32)
    shuffle = shuffle_ref[...].astype(f32)
    block_of = jnp.sum(jnp.where(eye, shuffle, 0.0), axis=1, keepdims=True)
    count_of = jnp.sum(jnp.where(block_of == lane_f, counts, 0.0), axis=1, keepdims=True)
    count_row = jnp.sum(jnp.where(eye, count_of, 0.0), axis=0, keepdims=True)
    ahead = (count_row > count_of) | ((count_row == count_of) & (lane < row))
    rank = jnp.sum(jnp.where(ahead, 1.0, 0.0), axis=1, keepdims=True)
    here = rank == lane_f
    lines = [jnp.sum(jnp.where(here, v, 0.0), axis=0, keepdims=True) for v in (place, block_of, count_of)]
    plan_ref[...] = jnp.concatenate(lines + [jnp.zeros((5, blocks), f32)], 0).astype(jnp.int32)

    for p, copy in enumerate(slab_means, 1):
        copy.wait()
        source = lax.rem(j - p + COLUMNS, COLUMNS)
        forwards += forward(p, near_ref.at[COLUMNS + source], source)

    def tabulate(highs):
        for k, h in enumerate(highs):
            parts = split(jnp.concatenate([near_ref[2 * h], near_ref[2 * h + 1]], 1))
            for piece in range(2):
                table_ref[piece, k * ROWS : (k + 1) * ROWS] = parts[piece]

    def pick(t, slot, highs):
        rows = len(highs) * ROWS
        pick_ref[slot, :rows] = mm(table_ref[0, :rows], low_ref[t]) + mm(table_ref[1, :rows], low_ref[t])

    def choose(t, slot, highs, b, mean):
        base = pl.multiple_of(t * TILE, TILE)
        high = (cell_ref[pl.ds(base, TILE), :] - first) >> 8
        high_row = jnp.broadcast_to(high[b : b + 1, :], (ROWS, LANES))
        lanes = slice(b * LANES, (b + 1) * LANES)
        for k, h in enumerate(highs):
            mean = jnp.where(high_row == h, pick_ref[slot, k * ROWS : (k + 1) * ROWS, lanes], mean)
        return mean

    tabulate(own_highs)

    def own_lookup(u, carry):
        for slot in range(2):
            t = 2 * u + slot
            pick(t, slot, own_highs)
            for b in range(TILE):
                state_ref[t * TILE + b] = choose(t, slot, own_highs, b, jnp.zeros((ROWS, LANES), f32))
        return carry

    lax.fori_loop(0, tiles // 2, own_lookup, 0)
    for copy in forwards:
        copy.wait()

    tabulate(other_highs)

    def other_lookup(u, carry):
        for slot in range(2):
            t = 2 * u + slot
            base = pl.multiple_of(t * TILE, TILE)
            pick(t, slot, other_highs)
            decay = jnp.exp(-rate_ref[pl.ds(base, TILE), :])
            for b in range(TILE):
                mean = choose(t, slot, other_highs, b, state_ref[base + b])[:NS]
                state_ref[base + b, :NS] = mean + (comp_ref[:, base + b, :] - mean) * decay[b : b + 1, :]
                state_ref[base + b, NS:] = jnp.zeros((ROWS - NS, LANES), f32)
        return carry

    lax.fori_loop(0, tiles // 2, other_lookup, 0)


def gather(n_gx, composition, mass, rate, cell, counts, shuffle, packed, stoichiometry):
    blocks = mass.shape[0]
    dma = pltpu.SemaphoreType.DMA
    piece = (COLUMNS, ROWS, CELL_DEV)
    return pl.pallas_call(
        functools.partial(gather_kernel, n_gx),
        out_shape=(
            jax.ShapeDtypeStruct((blocks, ROWS, LANES), f32),
            jax.ShapeDtypeStruct((n_gx * COLUMNS, ROWS, LANES), f32),
            jax.ShapeDtypeStruct((8, blocks), jnp.int32),
        ),
        in_specs=[VMEM] * 8,
        out_specs=(VMEM,) * 3,
        scratch_shapes=[
            pltpu.VMEM((blocks // TILE, 2 * ROWS, TILE * LANES), bf16),
            pltpu.VMEM((blocks // TILE, LOW, TILE * LANES), bf16),
            pltpu.VMEM((2, HIGHS * 2 * ROWS * 2 // 3, TILE * LANES), bf16),
            pltpu.VMEM((HIGHS * 2 * ROWS * 2 // 3, LOW), f32),
            pltpu.VMEM((2, HIGHS * ROWS * 2 // 3, TILE * LANES), f32),
            pltpu.VMEM((2, HIGHS * ROWS * 2 // 3, LOW), bf16),
            pltpu.VMEM((2 * COLUMNS, ROWS, CELL_DEV), f32),
            pltpu.VMEM((2, *piece), f32),
            pltpu.VMEM(piece, f32),
            pltpu.VMEM(piece, f32),
            pltpu.VMEM((ROWS, CELL_DEV), f32),
            pltpu.VMEM((3 * COLUMNS, ROWS, CELL_DEV), f32),
            pltpu.VMEM((COLUMNS, n_gx, PACK, LANES), f32),
            pltpu.VMEM((3 * LANES, NS // PACK * LANES), f32),
            dma((2,)), dma((2,)), *[dma((COLUMNS,))] * 8,
            dma((n_gx,)), dma((n_gx,)), dma((COLUMNS,)), dma((COLUMNS,)),
        ],
        compiler_params=pltpu.CompilerParams(
            collective_id=0, has_side_effects=True, vmem_limit_bytes=48 << 20
        ),
    )(composition, mass, rate, cell, counts, shuffle, packed, stoichiometry)


def react_kernel(plan_ref, state_ref, rates_ref, mats_ref, out_ref, pair_ref, turn_ref):
    blocks = state_ref.shape[0]
    turn_ref[...] = jnp.zeros_like(turn_ref)
    upper, lower = (v.astype(f32) for v in split(rates_ref[...]))
    for k, piece in enumerate((upper, upper, lower)):
        turn_ref[k * ROWS : k * ROWS + NS, :NR] = piece
    rates = turn_ref[...].T[:STEPS, : 3 * ROWS].astype(bf16)
    lane = lax.broadcasted_iota(jnp.int32, (ROWS, LANES), 1)

    def group(g, carry):
        at = [g * GROUP + b for b in range(GROUP)]
        block = [plan_ref[1, a] for a in at]
        need = [plan_ref[2, a] for a in at]
        for b in range(GROUP):
            upper, lower = (v.astype(f32) for v in split(mats_ref[plan_ref[0, at[b]]]))
            turned = pltpu.roll(upper, STEPS, 1)
            head = jnp.where(lane < STEPS, upper, turned)
            tail = jnp.where(lane < 2 * STEPS - LANES, turned, 0.0)
            pair_ref[b, :, :LANES] = jnp.concatenate([head, lower], 0).astype(bf16)
            pair_ref[b, :, LANES:] = jnp.concatenate([tail, jnp.zeros((ROWS, LANES), f32)], 0).astype(bf16)

        def section(s, states):
            x = jnp.concatenate(states, 1)
            upper = x.astype(bf16).astype(f32)
            progress = jnp.tanh(mm(rates, jnp.concatenate([upper, x - upper, upper], 0).astype(bf16)))
            upper = progress.astype(bf16).astype(f32)
            progress = jnp.concatenate([upper, progress - upper], 0).astype(bf16)
            products = [
                mm(
                    pair_ref[b : b + 2].reshape(4 * ROWS, 2 * LANES)[:, : 2 * STEPS],
                    progress[:, b * LANES : (b + 2) * LANES],
                )
                for b in range(0, GROUP, 2)
            ]
            after = []
            for b, y in zip(range(0, GROUP, 2), products):
                first_change = y[:24, :LANES] + y[24:48, :LANES]
                second_change = y[48:72, LANES:] + y[72:, LANES:]
                after.append(jnp.where(s < need[b], states[b] + first_change, states[b]))
                after.append(jnp.where(s < need[b + 1], states[b + 1] + second_change, states[b + 1]))
            return tuple(after)

        states = lax.fori_loop(0, need[0], section, tuple(state_ref[b] for b in block))
        for b in range(GROUP):
            out_ref[:, block[b], :] = states[b][:NS]
        return carry

    lax.fori_loop(0, blocks // GROUP, group, 0)


def react(plan, state, rates, mats):
    blocks = state.shape[0]
    return pl.pallas_call(
        react_kernel,
        out_shape=jax.ShapeDtypeStruct((NS, blocks, LANES), f32),
        in_specs=[SMEM] + [VMEM] * 3,
        out_specs=VMEM,
        scratch_shapes=[
            pltpu.VMEM((GROUP, 2 * ROWS, 2 * LANES), bf16),
            pltpu.VMEM((LANES, LANES), f32),
        ],
        compiler_params=pltpu.CompilerParams(vmem_limit_bytes=30 << 20),
    )(plan, state, rates, mats)


def local(
    n_gx, composition, particle_mass, mixing_rate, cell_index, section_counts,
    block_shuffle, batch_inverse, rate_exponents, stoichiometry,
):
    packed = jnp.pad(batch_inverse[0], ((0, 0), (0, ROWS - NS)))
    packed = packed.reshape(NS // PACK, PACK, ROWS).transpose(1, 0, 2).reshape(PACK, NS // PACK * ROWS)
    packed = jnp.pad(packed, ((0, 0), (0, LANES - NS // PACK * ROWS)))
    state, mats, plan = gather(
        n_gx, composition.transpose(1, 0, 2), particle_mass, mixing_rate, cell_index,
        section_counts[None], block_shuffle, packed, stoichiometry,
    )
    return react(plan, state, rate_exponents.T, mats).transpose(1, 0, 2)


def solution(mesh):
    both = ("gx", "yz")
    in_specs = (
        P(both, None, None), P(both, None), P(both, None), P(both, None), P(both),
        P(both, None), P(both, None, None), P(), P(),
    )
    return jax.shard_map(
        functools.partial(local, mesh.shape["gx"]),
        mesh=mesh, in_specs=in_specs, out_specs=P(both, None, None), check_vma=False,
    )
```

```python
import functools

import jax
import jax.numpy as jnp
from jax import lax
from jax.experimental import pallas as pl
from jax.experimental.pallas import tpu as pltpu
from jax.sharding import PartitionSpec as P

f32, bf16 = jnp.float32, jnp.bfloat16
MESH = pl.DeviceIdType.MESH
VMEM = pl.BlockSpec(memory_space=pltpu.VMEM)
SMEM = pl.BlockSpec(memory_space=pltpu.SMEM)
HBM = pl.BlockSpec(memory_space=pltpu.HBM)

NS, NR, LANES = 20, 84, 128
CELL_DEV = 128
COLUMNS = 16
SLAB = CELL_DEV * COLUMNS
LOW = 256
HIGHS = 3 * SLAB // LOW
ROWS = 24
STEPS = 88
TILE = 8
GROUP = 32
STEP_SIZE = 0.25
PACK = 4


def split(x):
    upper = x.astype(bf16)
    return upper, (x - upper.astype(f32)).astype(bf16)


def mm(a, b):
    return jnp.dot(a, b, preferred_element_type=f32)


def gather_kernel(
    n_gx, *refs,
):
    args, refs = refs[:8], refs[8:]
    outs = refs[:3]
    comp_ref, mass_ref, rate_ref, cell_ref, counts_ref, shuffle_ref, inverse_ref, stoich_ref = refs[3:11]
    (
        state_ref, mats_ref, plan_ref, fetch_sem, store_sem, square_ref,
        value_ref, low_ref, spread_ref, acc_ref, pick_ref, table_ref, part_ref, halo_ref, own_ref, sums_ref,
        mine_ref, near_ref, batch_ref, wide_ref,
        halo_send, halo_recv, sum_send, sum_recv, mean_send, mean_recv, left_send, left_recv,
        right_send, right_recv, row_send, row_recv, batch_send, batch_recv,
    ) = refs[11:]
    fetches = [
        pltpu.make_async_copy(src, dst, fetch_sem.at[k])
        for k, (src, dst) in enumerate(zip(args, refs[3:11]))
    ]
    for copy in fetches:
        copy.start()
    blocks = mass_ref.shape[0]
    tiles = blocks // TILE
    i, j = lax.axis_index("gx"), lax.axis_index("yz")
    left, right = lax.rem(i + n_gx - 1, n_gx), lax.rem(i + 1, n_gx)
    first = (i - 1) * SLAB
    iota = lax.broadcasted_iota(jnp.int32, (LOW, LANES), 0).astype(f32).astype(bf16)
    one, zero = jnp.ones((), bf16), jnp.zeros((), bf16)
    own_highs = range(HIGHS // 3, 2 * HIGHS // 3)
    other_highs = [h for h in range(HIGHS) if h not in own_highs]

    def column(p):
        return lax.rem(j + p, COLUMNS)

    def gx_peer(p):
        return lax.rem(i + p, n_gx)

    def send(src, dst, send_sem, recv_sem, target):
        copy = pltpu.make_async_remote_copy(
            src_ref=src, dst_ref=dst, send_sem=send_sem, recv_sem=recv_sem,
            device_id=target, device_id_type=MESH,
        )
        copy.start()
        return copy

    barrier = pltpu.get_barrier_semaphore()
    peers = [(gx_peer(p), j) for p in range(1, n_gx)] + [(i, column(p)) for p in range(1, COLUMNS)]
    for target in peers:
        pl.semaphore_signal(barrier, inc=1, device_id=target, device_id_type=MESH)
    acc_ref[...] = jnp.zeros_like(acc_ref)
    square_ref[...] = jnp.zeros_like(square_ref)
    for copy in fetches:
        copy.wait()

    square_ref[:NS, :NS] = inverse_ref[:, 0, :]
    packed = square_ref[:PACK]
    for c in range(1, NS // PACK):
        packed = packed + pltpu.roll(square_ref[PACK * c : PACK * (c + 1)], c * ROWS, 1)
    batch_ref[j, i] = packed

    def prepare(t):
        base = pl.multiple_of(t * TILE, TILE)
        low = ((cell_ref[pl.ds(base, TILE), :] - first) & (LOW - 1)).astype(f32)
        masses = mass_ref[pl.ds(base, TILE), :]
        for b in range(TILE):
            lanes = slice(b * LANES, (b + 1) * LANES)
            mass = masses[b : b + 1, :]
            value = jnp.concatenate(
                [comp_ref[:, base + b, :] * mass, mass, jnp.zeros((ROWS - NS - 1, LANES), f32)], 0
            )
            upper = value.astype(bf16).astype(f32)
            value_ref[t, :, lanes] = jnp.concatenate([upper, value - upper], 0).astype(bf16)
            low_row = jnp.broadcast_to(low[b : b + 1, :], (LOW, LANES)).astype(bf16)
            low_ref[t, :, lanes] = jnp.where(low_row == iota, one, zero)

    def spread(t, slot, highs):
        base = pl.multiple_of(t * TILE, TILE)
        high = ((cell_ref[pl.ds(base, TILE), :] - first) >> 8).astype(f32)
        for b in range(TILE):
            lanes = slice(b * LANES, (b + 1) * LANES)
            values = value_ref[t, :, lanes]
            high_row = jnp.broadcast_to(high[b : b + 1, :], (2 * ROWS, LANES)).astype(bf16)
            for k, h in enumerate(highs):
                spread_ref[slot, k * 2 * ROWS : (k + 1) * 2 * ROWS, lanes] = jnp.where(
                    high_row == jnp.asarray(h, bf16), values, zero
                )

    def accumulate(t, slot, highs):
        rows = len(highs) * 2 * ROWS
        acc_ref[:rows] += lax.dot_general(
            spread_ref[slot, :rows], low_ref[t], (((1,), (1,)), ((), ())), preferred_element_type=f32
        )

    def owners(highs):
        for k, h in enumerate(highs):
            total = acc_ref[k * 48 : k * 48 + 24, :] + acc_ref[k * 48 + 24 : k * 48 + 48, :]
            yield k, total[:, :CELL_DEV], total[:, CELL_DEV:]


    def other_tiles(u, carry):
        for slot in range(2):
            prepare(2 * u + slot)
            spread(2 * u + slot, slot, other_highs)
            accumulate(2 * u + slot, slot, other_highs)
        return carry

    lax.fori_loop(0, tiles // 2, other_tiles, 0)
    for k, even, odd in owners(other_highs):
        part_ref[2 * k] = even
        part_ref[2 * k + 1] = odd
    acc_ref[...] = jnp.zeros_like(acc_ref)

    pl.semaphore_wait(barrier, len(peers))
    halos = [
        send(part_ref.at[pl.ds(0, COLUMNS)], halo_ref.at[1], halo_send.at[0], halo_recv.at[0], (left, j)),
        send(part_ref.at[pl.ds(COLUMNS, COLUMNS)], halo_ref.at[0], halo_send.at[1], halo_recv.at[1], (right, j)),
    ]
    rows = [
        send(batch_ref.at[j, i], batch_ref.at[j, i], row_send.at[p], row_recv.at[p], (gx_peer(p), j))
        for p in range(1, n_gx)
    ]

    def own_tiles(u, carry):
        for slot in range(2):
            spread(2 * u + slot, slot, own_highs)
            accumulate(2 * u + slot, slot, own_highs)
        return carry

    lax.fori_loop(0, tiles // 4, own_tiles, 0)
    for copy in rows:
        copy.wait()
    batches = [
        send(batch_ref.at[j], batch_ref.at[j], batch_send.at[p], batch_recv.at[p], (i, column(p)))
        for p in range(1, COLUMNS)
    ]
    lax.fori_loop(tiles // 4, tiles // 2, own_tiles, 0)
    for copy in halos:
        copy.wait()
    for k, even, odd in owners(own_highs):
        own_ref[2 * k] = even + halo_ref[0, 2 * k] + halo_ref[1, 2 * k]
        own_ref[2 * k + 1] = odd + halo_ref[0, 2 * k + 1] + halo_ref[1, 2 * k + 1]

    partials = [
        send(own_ref.at[column(p)], sums_ref.at[p], sum_send.at[p], sum_recv.at[p], (i, column(p)))
        for p in range(1, COLUMNS)
    ]

    wide_ref[...] = jnp.zeros_like(wide_ref)
    upper, lower = (v.astype(f32) for v in split(STEP_SIZE * stoich_ref[...]))
    for c in range(NS // PACK):
        lanes = slice(c * LANES, c * LANES + NR)
        for k, piece in enumerate((upper, lower, upper)):
            wide_ref[k * LANES + c * ROWS : k * LANES + c * ROWS + NS, lanes] = piece
    wide = wide_ref[...].astype(bf16)
    for copy in batches:
        copy.wait()
    batch_total = n_gx * COLUMNS
    for t in range(PACK):
        upper, lower = split(batch_ref[:, :, t, :].reshape(batch_total, LANES))
        product = mm(jnp.concatenate([upper, upper, lower], 1), wide)
        for c in range(NS // PACK):
            mats_ref[:, PACK * c + t, :] = product[:, c * LANES : (c + 1) * LANES]
    for r in range(NS, ROWS):
        mats_ref[:, r, :] = jnp.zeros((batch_total, LANES), f32)
    stores = [pltpu.make_async_copy(mats_ref, outs[1], store_sem.at[tiles // 2])]
    stores[0].start()

    total = own_ref[j]
    for p, copy in enumerate(partials, 1):
        copy.wait()
        total = total + sums_ref[p]
    means = total[:NS] / total[NS : NS + 1]
    mine_ref[...] = jnp.concatenate([means, jnp.zeros((ROWS - NS, CELL_DEV), f32)], 0)

    slab_means = [
        send(mine_ref, near_ref.at[COLUMNS + j], mean_send.at[p], mean_recv.at[p], (i, column(p)))
        for p in range(1, COLUMNS)
    ]
    near_ref[COLUMNS + j] = mine_ref[...]

    def forward(p, src, at):
        return [
            send(src, near_ref.at[2 * COLUMNS + at], left_send.at[p], left_recv.at[p], (left, j)),
            send(src, near_ref.at[at], right_send.at[p], right_recv.at[p], (right, j)),
        ]

    forwards = forward(0, mine_ref, j)

    row = lax.broadcasted_iota(jnp.int32, (blocks, blocks), 0)
    lane = lax.broadcasted_iota(jnp.int32, (blocks, blocks), 1)
    lane_f = lane.astype(f32)
    place = ((row % COLUMNS) * (blocks // COLUMNS) + row // COLUMNS).astype(f32)
    eye = row == lane
    counts = counts_ref[...].astype(f32)
    shuffle = shuffle_ref[...].astype(f32)
    block_of = jnp.sum(jnp.where(eye, shuffle, 0.0), axis=1, keepdims=True)
    count_of = jnp.sum(jnp.where(block_of == lane_f, counts, 0.0), axis=1, keepdims=True)
    count_row = jnp.sum(jnp.where(eye, count_of, 0.0), axis=0, keepdims=True)
    ahead = (count_row > count_of) | ((count_row == count_of) & (lane < row))
    rank = jnp.sum(jnp.where(ahead, 1.0, 0.0), axis=1, keepdims=True)
    here = rank == lane_f
    lines = [jnp.sum(jnp.where(here, v, 0.0), axis=0, keepdims=True) for v in (place, block_of, count_of)]
    plan_ref[...] = jnp.concatenate(lines + [jnp.zeros((5, blocks), f32)], 0).astype(jnp.int32)
    stores.append(pltpu.make_async_copy(plan_ref, outs[2], store_sem.at[tiles // 2 + 1]))
    stores[1].start()

    for p, copy in enumerate(slab_means, 1):
        copy.wait()
        source = lax.rem(j - p + COLUMNS, COLUMNS)
        forwards += forward(p, near_ref.at[COLUMNS + source], source)

    def tabulate(highs):
        for k, h in enumerate(highs):
            parts = split(jnp.concatenate([near_ref[2 * h], near_ref[2 * h + 1]], 1))
            for piece in range(2):
                table_ref[piece, k * ROWS : (k + 1) * ROWS] = parts[piece]

    def pick(t, slot, highs):
        rows = len(highs) * ROWS
        pick_ref[slot, :rows] = mm(table_ref[0, :rows], low_ref[t]) + mm(table_ref[1, :rows], low_ref[t])

    def choose(t, slot, highs, b, mean):
        base = pl.multiple_of(t * TILE, TILE)
        high = (cell_ref[pl.ds(base, TILE), :] - first) >> 8
        high_row = jnp.broadcast_to(high[b : b + 1, :], (ROWS, LANES))
        lanes = slice(b * LANES, (b + 1) * LANES)
        for k, h in enumerate(highs):
            mean = jnp.where(high_row == h, pick_ref[slot, k * ROWS : (k + 1) * ROWS, lanes], mean)
        return mean

    tabulate(own_highs)

    def own_lookup(u, carry):
        for slot in range(2):
            t = 2 * u + slot
            pick(t, slot, own_highs)
            for b in range(TILE):
                state_ref[t * TILE + b] = choose(t, slot, own_highs, b, jnp.zeros((ROWS, LANES), f32))
        return carry

    lax.fori_loop(0, tiles // 2, own_lookup, 0)
    for copy in forwards:
        copy.wait()

    tabulate(other_highs)

    def other_lookup(u, carry):
        for slot in range(2):
            t = 2 * u + slot
            base = pl.multiple_of(t * TILE, TILE)
            pick(t, slot, other_highs)
            decay = jnp.exp(-rate_ref[pl.ds(base, TILE), :])
            for b in range(TILE):
                mean = choose(t, slot, other_highs, b, state_ref[base + b])[:NS]
                state_ref[base + b, :NS] = mean + (comp_ref[:, base + b, :] - mean) * decay[b : b + 1, :]
                state_ref[base + b, NS:] = jnp.zeros((ROWS - NS, LANES), f32)
        store_state(u).start()
        return carry

    def store_state(u):
        part = pl.ds(pl.multiple_of(u * 2 * TILE, 2 * TILE), 2 * TILE)
        return pltpu.make_async_copy(state_ref.at[part], outs[0].at[part], store_sem.at[u])

    lax.fori_loop(0, tiles // 2, other_lookup, 0)
    for copy in stores:
        copy.wait()
    for u in range(tiles // 2):
        store_state(u).wait()


def gather(n_gx, *args):
    blocks = args[1].shape[0]
    dma = pltpu.SemaphoreType.DMA
    piece = (COLUMNS, ROWS, CELL_DEV)
    outs = (
        jax.ShapeDtypeStruct((blocks, ROWS, LANES), f32),
        jax.ShapeDtypeStruct((n_gx * COLUMNS, ROWS, LANES), f32),
        jax.ShapeDtypeStruct((8, blocks), jnp.int32),
    )
    return pl.pallas_call(
        functools.partial(gather_kernel, n_gx),
        out_shape=outs,
        in_specs=[HBM] * 8,
        out_specs=(HBM,) * 3,
        scratch_shapes=[
            *[pltpu.VMEM(a.shape, a.dtype) for a in (*args, *outs)],
            dma((len(args),)),
            dma((blocks // TILE // 2 + 2,)),
            pltpu.VMEM((ROWS, LANES), f32),
            pltpu.VMEM((blocks // TILE, 2 * ROWS, TILE * LANES), bf16),
            pltpu.VMEM((blocks // TILE, LOW, TILE * LANES), bf16),
            pltpu.VMEM((2, HIGHS * 2 * ROWS * 2 // 3, TILE * LANES), bf16),
            pltpu.VMEM((HIGHS * 2 * ROWS * 2 // 3, LOW), f32),
            pltpu.VMEM((2, HIGHS * ROWS * 2 // 3, TILE * LANES), f32),
            pltpu.VMEM((2, HIGHS * ROWS * 2 // 3, LOW), bf16),
            pltpu.VMEM((2 * COLUMNS, ROWS, CELL_DEV), f32),
            pltpu.VMEM((2, *piece), f32),
            pltpu.VMEM(piece, f32),
            pltpu.VMEM(piece, f32),
            pltpu.VMEM((ROWS, CELL_DEV), f32),
            pltpu.VMEM((3 * COLUMNS, ROWS, CELL_DEV), f32),
            pltpu.VMEM((COLUMNS, n_gx, PACK, LANES), f32),
            pltpu.VMEM((3 * LANES, NS // PACK * LANES), f32),
            dma((2,)), dma((2,)), *[dma((COLUMNS,))] * 8,
            dma((n_gx,)), dma((n_gx,)), dma((COLUMNS,)), dma((COLUMNS,)),
        ],
        compiler_params=pltpu.CompilerParams(
            collective_id=0, has_side_effects=True, vmem_limit_bytes=60 << 20
        ),
    )(*args)


def react_kernel(plan_ref, *refs):
    args, (out_ref, state_ref, rates_ref, mats_ref, fetch_sem, pair_ref, turn_ref) = refs[:3], refs[3:]
    fetches = [
        pltpu.make_async_copy(src, dst, fetch_sem.at[k])
        for k, (src, dst) in enumerate(zip(args, (state_ref, rates_ref, mats_ref)))
    ]
    for copy in fetches:
        copy.start()
    blocks = state_ref.shape[0]
    fetches[1].wait()
    turn_ref[...] = jnp.zeros_like(turn_ref)
    upper, lower = (v.astype(f32) for v in split(rates_ref[...]))
    for k, piece in enumerate((upper, upper, lower)):
        turn_ref[k * ROWS : k * ROWS + NS, :NR] = piece
    rates = turn_ref[...].T[:STEPS, : 3 * ROWS].astype(bf16)
    lane = lax.broadcasted_iota(jnp.int32, (ROWS, LANES), 1)
    fetches[0].wait()
    fetches[2].wait()

    def group(g, carry):
        at = [g * GROUP + b for b in range(GROUP)]
        block = [plan_ref[1, a] for a in at]
        need = [plan_ref[2, a] for a in at]
        for b in range(GROUP):
            upper, lower = (v.astype(f32) for v in split(mats_ref[plan_ref[0, at[b]]]))
            turned = pltpu.roll(upper, STEPS, 1)
            head = jnp.where(lane < STEPS, upper, turned)
            tail = jnp.where(lane < 2 * STEPS - LANES, turned, 0.0)
            pair_ref[b, :, :LANES] = jnp.concatenate([head, lower], 0).astype(bf16)
            pair_ref[b, :, LANES:] = jnp.concatenate([tail, jnp.zeros((ROWS, LANES), f32)], 0).astype(bf16)

        def section(s, states):
            x = jnp.concatenate(states, 1)
            upper = x.astype(bf16).astype(f32)
            progress = jnp.tanh(mm(rates, jnp.concatenate([upper, x - upper, upper], 0).astype(bf16)))
            upper = progress.astype(bf16).astype(f32)
            progress = jnp.concatenate([upper, progress - upper], 0).astype(bf16)
            products = [
                mm(
                    pair_ref[b : b + 2].reshape(4 * ROWS, 2 * LANES)[:, : 2 * STEPS],
                    progress[:, b * LANES : (b + 2) * LANES],
                )
                for b in range(0, GROUP, 2)
            ]
            after = []
            for b, y in zip(range(0, GROUP, 2), products):
                first_change = y[:24, :LANES] + y[24:48, :LANES]
                second_change = y[48:72, LANES:] + y[72:, LANES:]
                after.append(jnp.where(s < need[b], states[b] + first_change, states[b]))
                after.append(jnp.where(s < need[b + 1], states[b + 1] + second_change, states[b + 1]))
            return tuple(after)

        states = lax.fori_loop(0, need[0], section, tuple(state_ref[b] for b in block))
        for b in range(GROUP):
            out_ref[:, block[b], :] = states[b][:NS]
        return carry

    lax.fori_loop(0, blocks // GROUP, group, 0)


def react(plan, state, rates, mats):
    blocks = state.shape[0]
    return pl.pallas_call(
        react_kernel,
        out_shape=jax.ShapeDtypeStruct((NS, blocks, LANES), f32),
        in_specs=[SMEM] + [HBM] * 3,
        out_specs=VMEM,
        scratch_shapes=[
            *[pltpu.VMEM(a.shape, a.dtype) for a in (state, rates, mats)],
            pltpu.SemaphoreType.DMA((3,)),
            pltpu.VMEM((GROUP, 2 * ROWS, 2 * LANES), bf16),
            pltpu.VMEM((LANES, LANES), f32),
        ],
        compiler_params=pltpu.CompilerParams(vmem_limit_bytes=60 << 20),
    )(plan, state, rates, mats)


def local(
    n_gx, composition, particle_mass, mixing_rate, cell_index, section_counts,
    block_shuffle, batch_inverse, rate_exponents, stoichiometry,
):
    state, mats, plan = gather(
        n_gx, composition.transpose(1, 0, 2), particle_mass, mixing_rate, cell_index,
        section_counts[None], block_shuffle, batch_inverse.transpose(1, 0, 2), stoichiometry,
    )
    return react(plan, state, rate_exponents.T, mats).transpose(1, 0, 2)


def solution(mesh):
    both = ("gx", "yz")
    in_specs = (
        P(both, None, None), P(both, None), P(both, None), P(both, None), P(both),
        P(both, None), P(both, None, None), P(), P(),
    )
    return jax.shard_map(
        functools.partial(local, mesh.shape["gx"]),
        mesh=mesh, in_specs=in_specs, out_specs=P(both, None, None), check_vma=False,
    )
```

```python
import functools

import jax
import jax.numpy as jnp
from jax import lax
from jax.experimental import pallas as pl
from jax.experimental.pallas import tpu as pltpu
from jax.sharding import PartitionSpec as P

f32, bf16, f8 = jnp.float32, jnp.bfloat16, jnp.float8_e4m3fn
MESH = pl.DeviceIdType.MESH
VMEM = pl.BlockSpec(memory_space=pltpu.VMEM)
SMEM = pl.BlockSpec(memory_space=pltpu.SMEM)
HBM = pl.BlockSpec(memory_space=pltpu.HBM)

NS, NR, LANES = 20, 84, 128
CELL_DEV = 128
COLUMNS = 16
SLAB = CELL_DEV * COLUMNS
LOW = 256
HIGHS = 3 * SLAB // LOW
ROWS = 24
STEPS = 88
TILE = 8
GROUP = 16
STEP_SIZE = 0.25
PARTS = 64
TOP = 224.0
MASS_SCALE = 64.0
PACK = 4


def split(x):
    upper = x.astype(bf16)
    return upper, (x - upper.astype(f32)).astype(bf16)


def cut(x):
    first = x.astype(f8).astype(f32)
    second = (x - first).astype(f8).astype(f32)
    return first, second, x - first - second


def mm(a, b):
    return jnp.dot(a, b, preferred_element_type=f32)


def gather_kernel(
    n_gx, *refs,
):
    args, refs = refs[:8], refs[8:]
    outs = refs[:3]
    comp_ref, mass_ref, rate_ref, cell_ref, counts_ref, shuffle_ref, inverse_ref, stoich_ref = refs[3:11]
    (
        state_ref, mats_ref, plan_ref, fetch_sem, store_sem, square_ref,
        value_ref, low_ref, spread_ref, acc_ref, pick_ref, table_ref, wide_table_ref, part_ref, halo_ref, own_ref, sums_ref,
        mine_ref, near_ref, batch_ref, wide_ref, product_ref,
        halo_send, halo_recv, sum_send, sum_recv, mean_send, mean_recv, left_send, left_recv,
        right_send, right_recv, row_send, row_recv, batch_send, batch_recv,
    ) = refs[11:]
    fetches = [
        pltpu.make_async_copy(src, dst, fetch_sem.at[k])
        for k, (src, dst) in enumerate(zip(args, refs[3:11]))
    ]
    for copy in fetches:
        copy.start()
    blocks = mass_ref.shape[0]
    tiles = blocks // TILE
    i, j = lax.axis_index("gx"), lax.axis_index("yz")
    left, right = lax.rem(i + n_gx - 1, n_gx), lax.rem(i + 1, n_gx)
    first = (i - 1) * SLAB
    iota = lax.broadcasted_iota(jnp.int32, (LOW, LANES), 0).astype(f32).astype(bf16)
    one, zero = jnp.ones((), bf16), jnp.zeros((), bf16)
    own_highs = range(HIGHS // 3, 2 * HIGHS // 3)
    other_highs = [h for h in range(HIGHS) if h not in own_highs]

    def column(p):
        return lax.rem(j + p, COLUMNS)

    def gx_peer(p):
        return lax.rem(i + p, n_gx)

    def send(src, dst, send_sem, recv_sem, target):
        copy = pltpu.make_async_remote_copy(
            src_ref=src, dst_ref=dst, send_sem=send_sem, recv_sem=recv_sem,
            device_id=target, device_id_type=MESH,
        )
        copy.start()
        return copy

    barrier = pltpu.get_barrier_semaphore()
    peers = [(gx_peer(p), j) for p in range(1, n_gx)] + [(i, column(p)) for p in range(1, COLUMNS)]
    for target in peers:
        pl.semaphore_signal(barrier, inc=1, device_id=target, device_id_type=MESH)
    acc_ref[...] = jnp.zeros_like(acc_ref)
    square_ref[...] = jnp.zeros_like(square_ref)
    for copy in fetches:
        copy.wait()

    square_ref[:NS, :NS] = inverse_ref[:, 0, :]
    packed = square_ref[:PACK]
    for c in range(1, NS // PACK):
        packed = packed + pltpu.roll(square_ref[PACK * c : PACK * (c + 1)], c * ROWS, 1)
    batch_ref[j, i] = packed

    bound = jnp.max(jnp.abs(comp_ref[...]), keepdims=True).reshape(1, 1) * jnp.max(mass_ref[...], keepdims=True)
    bound = jnp.maximum(bound, 1e-30)
    scale, unscale = TOP / bound, bound / TOP

    def prepare(t):
        base = pl.multiple_of(t * TILE, TILE)
        low = ((cell_ref[pl.ds(base, TILE), :] - first) & (LOW - 1)).astype(f32)
        masses = mass_ref[pl.ds(base, TILE), :]
        for b in range(TILE):
            lanes = slice(b * LANES, (b + 1) * LANES)
            mass = masses[b : b + 1, :]
            value = cut(comp_ref[:, base + b, :] * (mass * scale))
            weight = cut(mass * MASS_SCALE)
            value_ref[t, :, lanes] = jnp.concatenate(
                [value[0], *weight, jnp.zeros((1, LANES), f32), value[1], value[2]], 0
            ).astype(bf16)
            low_row = jnp.broadcast_to(low[b : b + 1, :], (LOW, LANES)).astype(bf16)
            low_ref[t, :, lanes] = jnp.where(low_row == iota, one, zero).astype(f8)

    def spread(t, slot, highs):
        base = pl.multiple_of(t * TILE, TILE)
        high = ((cell_ref[pl.ds(base, TILE), :] - first) >> 8).astype(f32)
        for b in range(TILE):
            lanes = slice(b * LANES, (b + 1) * LANES)
            values = value_ref[t, :, lanes]
            high_row = jnp.broadcast_to(high[b : b + 1, :], (PARTS, LANES)).astype(bf16)
            for k, h in enumerate(highs):
                spread_ref[slot, k * PARTS : (k + 1) * PARTS, lanes] = jnp.where(
                    high_row == jnp.asarray(h, bf16), values, zero
                ).astype(f8)

    def accumulate(t, slot, highs):
        rows = len(highs) * PARTS
        acc_ref[:rows] += lax.dot_general(
            spread_ref[slot, :rows], low_ref[t], (((1,), (1,)), ((), ())), preferred_element_type=f32
        )

    def owners(highs):
        for k, h in enumerate(highs):
            sums = acc_ref[k * PARTS : (k + 1) * PARTS, :]
            value = (sums[:NS] + sums[ROWS : ROWS + NS] + sums[ROWS + NS :]) * unscale
            weight = (sums[NS : NS + 1] + sums[NS + 1 : NS + 2] + sums[NS + 2 : NS + 3]) * (1 / MASS_SCALE)
            total = jnp.concatenate([value, weight, jnp.zeros((ROWS - NS - 1, LOW), f32)], 0)
            yield k, total[:, :CELL_DEV], total[:, CELL_DEV:]


    def other_tiles(u, carry):
        for slot in range(2):
            prepare(2 * u + slot)
            spread(2 * u + slot, slot, other_highs)
            accumulate(2 * u + slot, slot, other_highs)
        return carry

    lax.fori_loop(0, tiles // 2, other_tiles, 0)
    for k, even, odd in owners(other_highs):
        part_ref[2 * k] = even
        part_ref[2 * k + 1] = odd
    acc_ref[...] = jnp.zeros_like(acc_ref)

    pl.semaphore_wait(barrier, len(peers))
    halos = [
        send(part_ref.at[pl.ds(0, COLUMNS)], halo_ref.at[1], halo_send.at[0], halo_recv.at[0], (left, j)),
        send(part_ref.at[pl.ds(COLUMNS, COLUMNS)], halo_ref.at[0], halo_send.at[1], halo_recv.at[1], (right, j)),
    ]
    rows = [
        send(batch_ref.at[j, i], batch_ref.at[j, i], row_send.at[p], row_recv.at[p], (gx_peer(p), j))
        for p in range(1, n_gx)
    ]

    def own_tiles(u, carry):
        for slot in range(2):
            spread(2 * u + slot, slot, own_highs)
            accumulate(2 * u + slot, slot, own_highs)
        return carry

    lax.fori_loop(0, tiles // 4, own_tiles, 0)
    for copy in rows:
        copy.wait()
    batches = [
        send(batch_ref.at[j], batch_ref.at[j], batch_send.at[p], batch_recv.at[p], (i, column(p)))
        for p in range(1, COLUMNS)
    ]
    lax.fori_loop(tiles // 4, tiles // 2, own_tiles, 0)
    for copy in halos:
        copy.wait()
    for k, even, odd in owners(own_highs):
        own_ref[2 * k] = even + halo_ref[0, 2 * k] + halo_ref[1, 2 * k]
        own_ref[2 * k + 1] = odd + halo_ref[0, 2 * k + 1] + halo_ref[1, 2 * k + 1]

    partials = [
        send(own_ref.at[column(p)], sums_ref.at[p], sum_send.at[p], sum_recv.at[p], (i, column(p)))
        for p in range(1, COLUMNS)
    ]

    wide_ref[...] = jnp.zeros_like(wide_ref)
    upper, lower = (v.astype(f32) for v in split(STEP_SIZE * stoich_ref[...]))
    for c in range(NS // PACK):
        for k, piece in enumerate((upper, lower, upper)):
            for start in (0, STEPS):
                lanes = slice(2 * c * LANES + start, 2 * c * LANES + start + NR)
                wide_ref[k * LANES + c * ROWS : k * LANES + c * ROWS + NS, lanes] = piece
    wide = wide_ref[...].astype(bf16)
    for copy in batches:
        copy.wait()
    batch_total = n_gx * COLUMNS
    for t in range(PACK):
        upper, lower = split(batch_ref[:, :, t, :].reshape(batch_total, LANES))
        product = mm(jnp.concatenate([upper, upper, lower], 1), wide)
        for c in range(NS // PACK):
            for side in range(2):
                at = (2 * c + side) * LANES
                product_ref[:, PACK * c + t, side * LANES : (side + 1) * LANES] = product[:, at : at + LANES]
    for r in range(NS, ROWS):
        product_ref[:, r, :] = jnp.zeros((batch_total, 2 * LANES), f32)
    once = lax.broadcasted_iota(jnp.int32, (ROWS, 2 * LANES), 1) < STEPS

    def pair(u, carry):
        for k in range(8):
            value = product_ref[8 * u + k]
            upper = value.astype(bf16).astype(f32)
            mats_ref[8 * u + k] = jnp.concatenate([upper, jnp.where(once, value - upper, 0.0)], 0).astype(bf16)
        return carry

    lax.fori_loop(0, batch_total // 8, pair, 0)
    stores = [pltpu.make_async_copy(mats_ref, outs[1], store_sem.at[tiles // 2])]
    stores[0].start()

    total = own_ref[j]
    for p, copy in enumerate(partials, 1):
        copy.wait()
        total = total + sums_ref[p]
    means = total[:NS] / total[NS : NS + 1]
    mine_ref[...] = jnp.concatenate([means, jnp.zeros((ROWS - NS, CELL_DEV), f32)], 0)

    slab_means = [
        send(mine_ref, near_ref.at[COLUMNS + j], mean_send.at[p], mean_recv.at[p], (i, column(p)))
        for p in range(1, COLUMNS)
    ]
    near_ref[COLUMNS + j] = mine_ref[...]

    def forward(p, src, at):
        return [
            send(src, near_ref.at[2 * COLUMNS + at], left_send.at[p], left_recv.at[p], (left, j)),
            send(src, near_ref.at[at], right_send.at[p], right_recv.at[p], (right, j)),
        ]

    forwards = forward(0, mine_ref, j)

    row = lax.broadcasted_iota(jnp.int32, (blocks, blocks), 0)
    lane = lax.broadcasted_iota(jnp.int32, (blocks, blocks), 1)
    lane_f = lane.astype(f32)
    place = ((row % COLUMNS) * (blocks // COLUMNS) + row // COLUMNS).astype(f32)
    eye = row == lane
    counts = counts_ref[...].astype(f32)
    shuffle = shuffle_ref[...].astype(f32)
    block_of = jnp.sum(jnp.where(eye, shuffle, 0.0), axis=1, keepdims=True)
    count_of = jnp.sum(jnp.where(block_of == lane_f, counts, 0.0), axis=1, keepdims=True)
    count_row = jnp.sum(jnp.where(eye, count_of, 0.0), axis=0, keepdims=True)
    ahead = (count_row > count_of) | ((count_row == count_of) & (lane < row))
    rank = jnp.sum(jnp.where(ahead, 1.0, 0.0), axis=1, keepdims=True)
    here = rank == lane_f
    lines = [jnp.sum(jnp.where(here, v, 0.0), axis=0, keepdims=True) for v in (place, block_of, count_of)]
    plan_ref[...] = jnp.concatenate(lines + [jnp.zeros((5, blocks), f32)], 0).astype(jnp.int32)
    stores.append(pltpu.make_async_copy(plan_ref, outs[2], store_sem.at[tiles // 2 + 1]))
    stores[1].start()

    for p, copy in enumerate(slab_means, 1):
        copy.wait()
        source = lax.rem(j - p + COLUMNS, COLUMNS)
        forwards += forward(p, near_ref.at[COLUMNS + source], source)

    def tabulate(highs):
        bound = jnp.zeros((ROWS, CELL_DEV), f32)
        for h in highs:
            bound = jnp.maximum(bound, jnp.maximum(jnp.abs(near_ref[2 * h]), jnp.abs(near_ref[2 * h + 1])))
        bound = jnp.maximum(jnp.max(bound, keepdims=True), 1e-30)
        for k, h in enumerate(highs):
            parts = cut(jnp.concatenate([near_ref[2 * h], near_ref[2 * h + 1]], 1) * (TOP / bound))
            for piece in range(3):
                wide_table_ref[piece, k * ROWS : (k + 1) * ROWS] = parts[piece]
        rows = len(highs) * ROWS
        table_ref[:, :rows] = wide_table_ref[:, :rows].astype(f8)
        return bound / TOP

    def pick(t, slot, highs):
        rows = len(highs) * ROWS
        pick_ref[slot, :rows] = sum(mm(table_ref[piece, :rows], low_ref[t]) for piece in range(3))

    def choose(t, slot, highs, b):
        base = pl.multiple_of(t * TILE, TILE)
        high = (cell_ref[pl.ds(base, TILE), :] - first) >> 8
        high_row = jnp.broadcast_to(high[b : b + 1, :], (ROWS, LANES))
        lanes = slice(b * LANES, (b + 1) * LANES)
        mean = jnp.zeros((ROWS, LANES), f32)
        for k, h in enumerate(highs):
            mean = jnp.where(high_row == h, pick_ref[slot, k * ROWS : (k + 1) * ROWS, lanes], mean)
        return mean

    own_unscale = tabulate(own_highs)

    def own_lookup(u, carry):
        for slot in range(2):
            t = 2 * u + slot
            pick(t, slot, own_highs)
            for b in range(TILE):
                state_ref[t * TILE + b] = choose(t, slot, own_highs, b) * own_unscale
        return carry

    lax.fori_loop(0, tiles // 2, own_lookup, 0)
    for copy in forwards:
        copy.wait()

    other_unscale = tabulate(other_highs)

    def other_lookup(u, carry):
        for slot in range(2):
            t = 2 * u + slot
            base = pl.multiple_of(t * TILE, TILE)
            pick(t, slot, other_highs)
            decay = jnp.exp(-rate_ref[pl.ds(base, TILE), :])
            for b in range(TILE):
                mean = (state_ref[base + b] + choose(t, slot, other_highs, b) * other_unscale)[:NS]
                state_ref[base + b, :NS] = mean + (comp_ref[:, base + b, :] - mean) * decay[b : b + 1, :]
                state_ref[base + b, NS:] = jnp.zeros((ROWS - NS, LANES), f32)
        store_state(u).start()
        return carry

    def store_state(u):
        part = pl.ds(pl.multiple_of(u * 2 * TILE, 2 * TILE), 2 * TILE)
        return pltpu.make_async_copy(state_ref.at[part], outs[0].at[part], store_sem.at[u])

    lax.fori_loop(0, tiles // 2, other_lookup, 0)
    for copy in stores:
        copy.wait()
    for u in range(tiles // 2):
        store_state(u).wait()


def gather(n_gx, *args):
    blocks = args[1].shape[0]
    dma = pltpu.SemaphoreType.DMA
    piece = (COLUMNS, ROWS, CELL_DEV)
    outs = (
        jax.ShapeDtypeStruct((blocks, ROWS, LANES), f32),
        jax.ShapeDtypeStruct((n_gx * COLUMNS, 2 * ROWS, 2 * LANES), bf16),
        jax.ShapeDtypeStruct((8, blocks), jnp.int32),
    )
    return pl.pallas_call(
        functools.partial(gather_kernel, n_gx),
        out_shape=outs,
        in_specs=[HBM] * 8,
        out_specs=(HBM,) * 3,
        scratch_shapes=[
            *[pltpu.VMEM(a.shape, a.dtype) for a in (*args, *outs)],
            dma((len(args),)),
            dma((blocks // TILE // 2 + 2,)),
            pltpu.VMEM((ROWS, LANES), f32),
            pltpu.VMEM((blocks // TILE, PARTS, TILE * LANES), bf16),
            pltpu.VMEM((blocks // TILE, LOW, TILE * LANES), f8),
            pltpu.VMEM((2, HIGHS * PARTS * 2 // 3, TILE * LANES), f8),
            pltpu.VMEM((HIGHS * PARTS * 2 // 3, LOW), f32),
            pltpu.VMEM((2, HIGHS * ROWS * 2 // 3, TILE * LANES), f32),
            pltpu.VMEM((3, HIGHS * ROWS * 2 // 3, LOW), f8),
            pltpu.VMEM((3, HIGHS * ROWS * 2 // 3, LOW), f32),
            pltpu.VMEM((2 * COLUMNS, ROWS, CELL_DEV), f32),
            pltpu.VMEM((2, *piece), f32),
            pltpu.VMEM(piece, f32),
            pltpu.VMEM(piece, f32),
            pltpu.VMEM((ROWS, CELL_DEV), f32),
            pltpu.VMEM((3 * COLUMNS, ROWS, CELL_DEV), f32),
            pltpu.VMEM((COLUMNS, n_gx, PACK, LANES), f32),
            pltpu.VMEM((3 * LANES, NS // PACK * 2 * LANES), f32),
            pltpu.VMEM((n_gx * COLUMNS, ROWS, 2 * LANES), f32),
            dma((2,)), dma((2,)), *[dma((COLUMNS,))] * 8,
            dma((n_gx,)), dma((n_gx,)), dma((COLUMNS,)), dma((COLUMNS,)),
        ],
        compiler_params=pltpu.CompilerParams(
            collective_id=0, has_side_effects=True, vmem_limit_bytes=60 << 20
        ),
    )(*args)


def react_kernel(plan_ref, *refs):
    args, (out_ref, state_ref, rates_ref, mats_ref, fetch_sem, pair_ref, half_ref, progress_ref, turn_ref) = refs[:3], refs[3:]
    fetches = [
        pltpu.make_async_copy(src, dst, fetch_sem.at[k])
        for k, (src, dst) in enumerate(zip(args, (state_ref, rates_ref, mats_ref)))
    ]
    for copy in fetches:
        copy.start()
    blocks = state_ref.shape[0]
    fetches[1].wait()
    turn_ref[...] = jnp.zeros_like(turn_ref)
    upper, lower = (v.astype(f32) for v in split(rates_ref[...]))
    for k, piece in enumerate((upper, upper, lower)):
        turn_ref[k * ROWS : k * ROWS + NS, :NR] = piece
    rates = turn_ref[...].T[:STEPS, : 3 * ROWS].astype(bf16)
    fetches[0].wait()
    fetches[2].wait()

    def progress(half):
        x = half_ref[half]
        upper = x.astype(bf16).astype(f32)
        value = jnp.tanh(mm(rates, jnp.concatenate([upper, x - upper, upper], 0).astype(bf16)))
        upper = value.astype(bf16).astype(f32)
        progress_ref[half] = jnp.concatenate([upper, value - upper], 0).astype(bf16)

    def change(half, s, need):
        products = [
            mm(
                pair_ref[half, b : b + 2].reshape(4 * ROWS, 2 * LANES)[:, : 2 * STEPS],
                progress_ref[half, :, b * LANES : (b + 2) * LANES],
            )
            for b in range(0, GROUP, 2)
        ]
        for b, y in zip(range(0, GROUP, 2), products):
            for c in range(2):
                lanes = slice((b + c) * LANES, (b + c + 1) * LANES)
                mine = y[48 * c : 48 * c + 48, c * LANES : (c + 1) * LANES]
                half_ref[half, :, lanes] += jnp.where(s < need[b + c], mine[:24] + mine[24:], 0.0)

    def two_groups(g, carry):
        block, need = [], []
        for half in range(2):
            at = [(2 * g + half) * GROUP + b for b in range(GROUP)]
            block.append([plan_ref[1, a] for a in at])
            need.append([plan_ref[2, a] for a in at])
            for b in range(GROUP):
                pair_ref[half, b] = mats_ref[plan_ref[0, at[b]]]
                half_ref[half, :, b * LANES : (b + 1) * LANES] = state_ref[block[half][b]]
        progress(0)

        def section(s, carry):
            change(0, s, need[0])
            progress(1)
            progress(0)
            change(1, s, need[1])
            return carry

        lax.fori_loop(0, need[0][0], section, 0)
        for half in range(2):
            for b in range(GROUP):
                out_ref[:, block[half][b], :] = half_ref[half, :NS, b * LANES : (b + 1) * LANES]
        return carry

    lax.fori_loop(0, blocks // (2 * GROUP), two_groups, 0)


def react(plan, state, rates, mats):
    blocks = state.shape[0]
    return pl.pallas_call(
        react_kernel,
        out_shape=jax.ShapeDtypeStruct((NS, blocks, LANES), f32),
        in_specs=[SMEM] + [HBM] * 3,
        out_specs=VMEM,
        scratch_shapes=[
            *[pltpu.VMEM(a.shape, a.dtype) for a in (state, rates, mats)],
            pltpu.SemaphoreType.DMA((3,)),
            pltpu.VMEM((2, GROUP, 2 * ROWS, 2 * LANES), bf16),
            pltpu.VMEM((2, ROWS, GROUP * LANES), f32),
            pltpu.VMEM((2, 2 * STEPS, GROUP * LANES), bf16),
            pltpu.VMEM((LANES, LANES), f32),
        ],
        compiler_params=pltpu.CompilerParams(vmem_limit_bytes=60 << 20),
    )(plan, state, rates, mats)


def local(
    n_gx, composition, particle_mass, mixing_rate, cell_index, section_counts,
    block_shuffle, batch_inverse, rate_exponents, stoichiometry,
):
    state, mats, plan = gather(
        n_gx, composition.transpose(1, 0, 2), particle_mass, mixing_rate, cell_index,
        section_counts[None], block_shuffle, batch_inverse.transpose(1, 0, 2), stoichiometry,
    )
    return react(plan, state, rate_exponents.T, mats).transpose(1, 0, 2)


def solution(mesh):
    both = ("gx", "yz")
    in_specs = (
        P(both, None, None), P(both, None), P(both, None), P(both, None), P(both),
        P(both, None), P(both, None, None), P(), P(),
    )
    return jax.shard_map(
        functools.partial(local, mesh.shape["gx"]),
        mesh=mesh, in_specs=in_specs, out_specs=P(both, None, None), check_vma=False,
    )
```

```python
import functools

import jax
import jax.numpy as jnp
from jax import lax
from jax.experimental import pallas as pl
from jax.experimental.pallas import tpu as pltpu
from jax.sharding import PartitionSpec as P

f32, bf16, f8 = jnp.float32, jnp.bfloat16, jnp.float8_e4m3fn
MESH = pl.DeviceIdType.MESH
VMEM = pl.BlockSpec(memory_space=pltpu.VMEM)
SMEM = pl.BlockSpec(memory_space=pltpu.SMEM)
HBM = pl.BlockSpec(memory_space=pltpu.HBM)

NS, NR, LANES = 20, 84, 128
CELL_DEV = 128
COLUMNS = 16
SLAB = CELL_DEV * COLUMNS
LOW = 256
HIGHS = 3 * SLAB // LOW
ROWS = 24
STEPS = 88
TILE = 8
GROUP = 32
STEP_SIZE = 0.25
PARTS = 64
TOP = 224.0
MASS_SCALE = 64.0
PACK = 4


def split(x):
    upper = x.astype(bf16)
    return upper, (x - upper.astype(f32)).astype(bf16)


def cut(x):
    first = x.astype(f8).astype(f32)
    second = (x - first).astype(f8).astype(f32)
    return first, second, x - first - second


def mm(a, b):
    return jnp.dot(a, b, preferred_element_type=f32)


def gather_kernel(
    n_gx, *refs,
):
    args, refs = refs[:8], refs[8:]
    outs = refs[:3]
    comp_ref, mass_ref, rate_ref, cell_ref, counts_ref, shuffle_ref, inverse_ref, stoich_ref = refs[3:11]
    (
        state_ref, mats_ref, plan_ref, fetch_sem, store_sem, square_ref,
        value_ref, low_ref, spread_ref, acc_ref, pick_ref, table_ref, wide_table_ref, part_ref, halo_ref, own_ref, sums_ref,
        mine_ref, near_ref, batch_ref, wide_ref, product_ref,
        halo_send, halo_recv, sum_send, sum_recv, mean_send, mean_recv, left_send, left_recv,
        right_send, right_recv, row_send, row_recv, batch_send, batch_recv,
    ) = refs[11:]
    fetches = [
        pltpu.make_async_copy(src, dst, fetch_sem.at[k])
        for k, (src, dst) in enumerate(zip(args, refs[3:11]))
    ]
    for copy in fetches:
        copy.start()
    blocks = mass_ref.shape[0]
    tiles = blocks // TILE
    i, j = lax.axis_index("gx"), lax.axis_index("yz")
    left, right = lax.rem(i + n_gx - 1, n_gx), lax.rem(i + 1, n_gx)
    first = (i - 1) * SLAB
    iota = lax.broadcasted_iota(jnp.int32, (LOW, LANES), 0).astype(f32).astype(bf16)
    one, zero = jnp.ones((), bf16), jnp.zeros((), bf16)
    own_highs = range(HIGHS // 3, 2 * HIGHS // 3)
    other_highs = [h for h in range(HIGHS) if h not in own_highs]

    def column(p):
        return lax.rem(j + p, COLUMNS)

    def gx_peer(p):
        return lax.rem(i + p, n_gx)

    def send(src, dst, send_sem, recv_sem, target):
        copy = pltpu.make_async_remote_copy(
            src_ref=src, dst_ref=dst, send_sem=send_sem, recv_sem=recv_sem,
            device_id=target, device_id_type=MESH,
        )
        copy.start()
        return copy

    barrier = pltpu.get_barrier_semaphore()
    peers = [(gx_peer(p), j) for p in range(1, n_gx)] + [(i, column(p)) for p in range(1, COLUMNS)]
    for target in peers:
        pl.semaphore_signal(barrier, inc=1, device_id=target, device_id_type=MESH)
    acc_ref[...] = jnp.zeros_like(acc_ref)
    square_ref[...] = jnp.zeros_like(square_ref)
    for copy in fetches:
        copy.wait()

    square_ref[:NS, :NS] = inverse_ref[:, 0, :]
    packed = square_ref[:PACK]
    for c in range(1, NS // PACK):
        packed = packed + pltpu.roll(square_ref[PACK * c : PACK * (c + 1)], c * ROWS, 1)
    batch_ref[j, i] = packed

    bound = jnp.max(jnp.abs(comp_ref[...]), keepdims=True).reshape(1, 1) * jnp.max(mass_ref[...], keepdims=True)
    bound = jnp.maximum(bound, 1e-30)
    scale, unscale = TOP / bound, bound / TOP

    def prepare(t):
        base = pl.multiple_of(t * TILE, TILE)
        low = ((cell_ref[pl.ds(base, TILE), :] - first) & (LOW - 1)).astype(f32)
        masses = mass_ref[pl.ds(base, TILE), :]
        for b in range(TILE):
            lanes = slice(b * LANES, (b + 1) * LANES)
            mass = masses[b : b + 1, :]
            value = cut(comp_ref[:, base + b, :] * (mass * scale))
            weight = cut(mass * MASS_SCALE)
            value_ref[t, :, lanes] = jnp.concatenate(
                [value[0], *weight, jnp.zeros((1, LANES), f32), value[1], value[2]], 0
            ).astype(bf16)
            low_row = jnp.broadcast_to(low[b : b + 1, :], (LOW, LANES)).astype(bf16)
            low_ref[t, :, lanes] = jnp.where(low_row == iota, one, zero).astype(f8)

    def spread(t, slot, highs):
        base = pl.multiple_of(t * TILE, TILE)
        high = ((cell_ref[pl.ds(base, TILE), :] - first) >> 8).astype(f32)
        for b in range(TILE):
            lanes = slice(b * LANES, (b + 1) * LANES)
            values = value_ref[t, :, lanes]
            high_row = jnp.broadcast_to(high[b : b + 1, :], (PARTS, LANES)).astype(bf16)
            for k, h in enumerate(highs):
                spread_ref[slot, k * PARTS : (k + 1) * PARTS, lanes] = jnp.where(
                    high_row == jnp.asarray(h, bf16), values, zero
                ).astype(f8)

    def accumulate(t, slot, highs):
        rows = len(highs) * PARTS
        acc_ref[:rows] += lax.dot_general(
            spread_ref[slot, :rows], low_ref[t], (((1,), (1,)), ((), ())), preferred_element_type=f32
        )

    def owners(highs):
        for k, h in enumerate(highs):
            sums = acc_ref[k * PARTS : (k + 1) * PARTS, :]
            value = (sums[:NS] + sums[ROWS : ROWS + NS] + sums[ROWS + NS :]) * unscale
            weight = (sums[NS : NS + 1] + sums[NS + 1 : NS + 2] + sums[NS + 2 : NS + 3]) * (1 / MASS_SCALE)
            total = jnp.concatenate([value, weight, jnp.zeros((ROWS - NS - 1, LOW), f32)], 0)
            yield k, total[:, :CELL_DEV], total[:, CELL_DEV:]


    def other_tiles(u, carry):
        for slot in range(2):
            prepare(2 * u + slot)
            spread(2 * u + slot, slot, other_highs)
            accumulate(2 * u + slot, slot, other_highs)
        return carry

    lax.fori_loop(0, tiles // 4, other_tiles, 0)
    pl.semaphore_wait(barrier, len(peers))
    rows = [
        send(batch_ref.at[j, i], batch_ref.at[j, i], row_send.at[p], row_recv.at[p], (gx_peer(p), j))
        for p in range(1, n_gx)
    ]
    lax.fori_loop(tiles // 4, tiles // 2, other_tiles, 0)
    for k, even, odd in owners(other_highs):
        part_ref[2 * k] = even
        part_ref[2 * k + 1] = odd
    acc_ref[...] = jnp.zeros_like(acc_ref)

    halos = [
        send(part_ref.at[pl.ds(0, COLUMNS)], halo_ref.at[1], halo_send.at[0], halo_recv.at[0], (left, j)),
        send(part_ref.at[pl.ds(COLUMNS, COLUMNS)], halo_ref.at[0], halo_send.at[1], halo_recv.at[1], (right, j)),
    ]
    for copy in rows:
        copy.wait()
    batches = [
        send(batch_ref.at[j], batch_ref.at[j], batch_send.at[p], batch_recv.at[p], (i, column(p)))
        for p in range(1, COLUMNS)
    ]

    def own_tiles(u, carry):
        for slot in range(2):
            spread(2 * u + slot, slot, own_highs)
            accumulate(2 * u + slot, slot, own_highs)
        return carry

    lax.fori_loop(0, tiles // 2, own_tiles, 0)

    row = lax.broadcasted_iota(jnp.int32, (blocks, blocks), 0)
    lane = lax.broadcasted_iota(jnp.int32, (blocks, blocks), 1)
    lane_f = lane.astype(f32)
    place = ((row % COLUMNS) * (blocks // COLUMNS) + row // COLUMNS).astype(f32)
    eye = row == lane
    counts = counts_ref[...].astype(f32)
    shuffle = shuffle_ref[...].astype(f32)
    block_of = jnp.sum(jnp.where(eye, shuffle, 0.0), axis=1, keepdims=True)
    count_of = jnp.sum(jnp.where(block_of == lane_f, counts, 0.0), axis=1, keepdims=True)
    count_row = jnp.sum(jnp.where(eye, count_of, 0.0), axis=0, keepdims=True)
    ahead = (count_row > count_of) | ((count_row == count_of) & (lane < row))
    rank = jnp.sum(jnp.where(ahead, 1.0, 0.0), axis=1, keepdims=True)
    here = rank == lane_f
    lines = [jnp.sum(jnp.where(here, v, 0.0), axis=0, keepdims=True) for v in (place, block_of, count_of)]
    plan_ref[...] = jnp.concatenate(lines + [jnp.zeros((5, blocks), f32)], 0).astype(jnp.int32)
    stores = [pltpu.make_async_copy(plan_ref, outs[2], store_sem.at[tiles // 2 + 1])]
    stores[0].start()

    for copy in halos:
        copy.wait()
    for k, even, odd in owners(own_highs):
        own_ref[2 * k] = even + halo_ref[0, 2 * k] + halo_ref[1, 2 * k]
        own_ref[2 * k + 1] = odd + halo_ref[0, 2 * k + 1] + halo_ref[1, 2 * k + 1]

    partials = [
        send(own_ref.at[column(p)], sums_ref.at[p], sum_send.at[p], sum_recv.at[p], (i, column(p)))
        for p in range(1, COLUMNS)
    ]

    wide_ref[...] = jnp.zeros_like(wide_ref)
    upper, lower = (v.astype(f32) for v in split(STEP_SIZE * stoich_ref[...]))
    for c in range(NS // PACK):
        for k, piece in enumerate((upper, lower, upper)):
            for start in (0, STEPS):
                lanes = slice(2 * c * LANES + start, 2 * c * LANES + start + NR)
                wide_ref[k * LANES + c * ROWS : k * LANES + c * ROWS + NS, lanes] = piece
    wide = wide_ref[...].astype(bf16)
    for copy in batches:
        copy.wait()
    batch_total = n_gx * COLUMNS
    for t in range(PACK):
        upper, lower = split(batch_ref[:, :, t, :].reshape(batch_total, LANES))
        product = mm(jnp.concatenate([upper, upper, lower], 1), wide)
        for c in range(NS // PACK):
            for side in range(2):
                at = (2 * c + side) * LANES
                product_ref[:, PACK * c + t, side * LANES : (side + 1) * LANES] = product[:, at : at + LANES]
    for r in range(NS, ROWS):
        product_ref[:, r, :] = jnp.zeros((batch_total, 2 * LANES), f32)
    total = own_ref[j]
    for p, copy in enumerate(partials, 1):
        copy.wait()
        total = total + sums_ref[p]
    means = total[:NS] / total[NS : NS + 1]
    mine_ref[...] = jnp.concatenate([means, jnp.zeros((ROWS - NS, CELL_DEV), f32)], 0)

    slab_means = [
        send(mine_ref, near_ref.at[COLUMNS + j], mean_send.at[p], mean_recv.at[p], (i, column(p)))
        for p in range(1, COLUMNS)
    ]
    near_ref[COLUMNS + j] = mine_ref[...]

    def forward(p, src, at):
        return [
            send(src, near_ref.at[2 * COLUMNS + at], left_send.at[p], left_recv.at[p], (left, j)),
            send(src, near_ref.at[at], right_send.at[p], right_recv.at[p], (right, j)),
        ]

    forwards = forward(0, mine_ref, j)

    once = lax.broadcasted_iota(jnp.int32, (ROWS, 2 * LANES), 1) < STEPS

    def pair(u, carry):
        for k in range(8):
            value = product_ref[8 * u + k]
            upper = value.astype(bf16).astype(f32)
            mats_ref[8 * u + k] = jnp.concatenate([upper, jnp.where(once, value - upper, 0.0)], 0).astype(bf16)
        return carry

    lax.fori_loop(0, batch_total // 8, pair, 0)
    stores.append(pltpu.make_async_copy(mats_ref, outs[1], store_sem.at[tiles // 2]))
    stores[1].start()

    for p, copy in enumerate(slab_means, 1):
        copy.wait()
        source = lax.rem(j - p + COLUMNS, COLUMNS)
        forwards += forward(p, near_ref.at[COLUMNS + source], source)

    def tabulate(highs):
        bound = jnp.zeros((ROWS, CELL_DEV), f32)
        for h in highs:
            bound = jnp.maximum(bound, jnp.maximum(jnp.abs(near_ref[2 * h]), jnp.abs(near_ref[2 * h + 1])))
        bound = jnp.maximum(jnp.max(bound, keepdims=True), 1e-30)
        for k, h in enumerate(highs):
            parts = cut(jnp.concatenate([near_ref[2 * h], near_ref[2 * h + 1]], 1) * (TOP / bound))
            for piece in range(3):
                wide_table_ref[piece, k * ROWS : (k + 1) * ROWS] = parts[piece]
        rows = len(highs) * ROWS
        table_ref[:, :rows] = wide_table_ref[:, :rows].astype(f8)
        return bound / TOP

    def pick(t, slot, highs):
        rows = len(highs) * ROWS
        pick_ref[slot, :rows] = sum(mm(table_ref[piece, :rows], low_ref[t]) for piece in range(3))

    def choose(t, slot, highs, b):
        base = pl.multiple_of(t * TILE, TILE)
        high = (cell_ref[pl.ds(base, TILE), :] - first) >> 8
        high_row = jnp.broadcast_to(high[b : b + 1, :], (ROWS, LANES))
        lanes = slice(b * LANES, (b + 1) * LANES)
        mean = jnp.zeros((ROWS, LANES), f32)
        for k, h in enumerate(highs):
            mean = jnp.where(high_row == h, pick_ref[slot, k * ROWS : (k + 1) * ROWS, lanes], mean)
        return mean

    own_unscale = tabulate(own_highs)

    def own_lookup(u, carry):
        for slot in range(2):
            t = 2 * u + slot
            pick(t, slot, own_highs)
            for b in range(TILE):
                state_ref[t * TILE + b] = choose(t, slot, own_highs, b) * own_unscale
        return carry

    lax.fori_loop(0, tiles // 2, own_lookup, 0)
    for copy in forwards:
        copy.wait()

    other_unscale = tabulate(other_highs)

    def other_lookup(u, carry):
        for slot in range(2):
            t = 2 * u + slot
            base = pl.multiple_of(t * TILE, TILE)
            pick(t, slot, other_highs)
            decay = jnp.exp(-rate_ref[pl.ds(base, TILE), :])
            for b in range(TILE):
                mean = (state_ref[base + b] + choose(t, slot, other_highs, b) * other_unscale)[:NS]
                state_ref[base + b, :NS] = mean + (comp_ref[:, base + b, :] - mean) * decay[b : b + 1, :]
                state_ref[base + b, NS:] = jnp.zeros((ROWS - NS, LANES), f32)
        store_state(u).start()
        return carry

    def store_state(u):
        part = pl.ds(pl.multiple_of(u * 2 * TILE, 2 * TILE), 2 * TILE)
        return pltpu.make_async_copy(state_ref.at[part], outs[0].at[part], store_sem.at[u])

    lax.fori_loop(0, tiles // 2, other_lookup, 0)
    for copy in stores:
        copy.wait()
    for u in range(tiles // 2):
        store_state(u).wait()


def gather(n_gx, *args):
    blocks = args[1].shape[0]
    dma = pltpu.SemaphoreType.DMA
    piece = (COLUMNS, ROWS, CELL_DEV)
    outs = (
        jax.ShapeDtypeStruct((blocks, ROWS, LANES), f32),
        jax.ShapeDtypeStruct((n_gx * COLUMNS, 2 * ROWS, 2 * LANES), bf16),
        jax.ShapeDtypeStruct((8, blocks), jnp.int32),
    )
    return pl.pallas_call(
        functools.partial(gather_kernel, n_gx),
        out_shape=outs,
        in_specs=[HBM] * 8,
        out_specs=(HBM,) * 3,
        scratch_shapes=[
            *[pltpu.VMEM(a.shape, a.dtype) for a in (*args, *outs)],
            dma((len(args),)),
            dma((blocks // TILE // 2 + 2,)),
            pltpu.VMEM((ROWS, LANES), f32),
            pltpu.VMEM((blocks // TILE, PARTS, TILE * LANES), bf16),
            pltpu.VMEM((blocks // TILE, LOW, TILE * LANES), f8),
            pltpu.VMEM((2, HIGHS * PARTS * 2 // 3, TILE * LANES), f8),
            pltpu.VMEM((HIGHS * PARTS * 2 // 3, LOW), f32),
            pltpu.VMEM((2, HIGHS * ROWS * 2 // 3, TILE * LANES), f32),
            pltpu.VMEM((3, HIGHS * ROWS * 2 // 3, LOW), f8),
            pltpu.VMEM((3, HIGHS * ROWS * 2 // 3, LOW), f32),
            pltpu.VMEM((2 * COLUMNS, ROWS, CELL_DEV), f32),
            pltpu.VMEM((2, *piece), f32),
            pltpu.VMEM(piece, f32),
            pltpu.VMEM(piece, f32),
            pltpu.VMEM((ROWS, CELL_DEV), f32),
            pltpu.VMEM((3 * COLUMNS, ROWS, CELL_DEV), f32),
            pltpu.VMEM((COLUMNS, n_gx, PACK, LANES), f32),
            pltpu.VMEM((3 * LANES, NS // PACK * 2 * LANES), f32),
            pltpu.VMEM((n_gx * COLUMNS, ROWS, 2 * LANES), f32),
            dma((2,)), dma((2,)), *[dma((COLUMNS,))] * 8,
            dma((n_gx,)), dma((n_gx,)), dma((COLUMNS,)), dma((COLUMNS,)),
        ],
        compiler_params=pltpu.CompilerParams(
            collective_id=0, has_side_effects=True, vmem_limit_bytes=60 << 20
        ),
    )(*args)


def react_kernel(plan_ref, *refs):
    args, (out_ref, state_ref, rates_ref, mats_ref, fetch_sem, turn_ref) = refs[:3], refs[3:]
    fetches = [
        pltpu.make_async_copy(src, dst, fetch_sem.at[k])
        for k, (src, dst) in enumerate(zip(args, (state_ref, rates_ref, mats_ref)))
    ]
    for copy in fetches:
        copy.start()
    blocks = state_ref.shape[0]
    turn_ref[...] = jnp.zeros_like(turn_ref)
    fetches[1].wait()
    upper, lower = (v.astype(f32) for v in split(rates_ref[...]))
    for k, piece in enumerate((upper, upper, lower)):
        turn_ref[k * ROWS : k * ROWS + NS, :NR] = piece
    rates = turn_ref[...].T[:STEPS, : 3 * ROWS].astype(bf16)
    fetches[0].wait()
    fetches[2].wait()

    def group(g, carry):
        at = [g * GROUP + b for b in range(GROUP)]
        batch, block, need = ([plan_ref[line, a] for a in at] for line in range(3))

        def section(s, states):
            x = jnp.concatenate(states, 1)
            upper = x.astype(bf16).astype(f32)
            progress = jnp.tanh(mm(rates, jnp.concatenate([upper, x - upper, upper], 0).astype(bf16)))
            upper = progress.astype(bf16).astype(f32)
            progress = jnp.concatenate([upper, progress - upper], 0).astype(bf16)
            products = [
                mm(
                    jnp.concatenate([mats_ref[batch[b]], mats_ref[batch[b + 1]]], 0)[:, : 2 * STEPS],
                    progress[:, b * LANES : (b + 2) * LANES],
                )
                for b in range(0, GROUP, 2)
            ]
            after = []
            for b, y in zip(range(0, GROUP, 2), products):
                for c in range(2):
                    mine = y[48 * c : 48 * c + 48, c * LANES : (c + 1) * LANES]
                    after.append(states[b + c] + jnp.where(s < need[b + c], mine[:24] + mine[24:], 0.0))
            return tuple(after)

        states = lax.fori_loop(0, need[0], section, tuple(state_ref[b] for b in block))
        for b in range(GROUP):
            out_ref[:, block[b], :] = states[b][:NS]
        return carry

    lax.fori_loop(0, blocks // GROUP, group, 0)


def react(plan, state, rates, mats):
    blocks = state.shape[0]
    return pl.pallas_call(
        react_kernel,
        out_shape=jax.ShapeDtypeStruct((NS, blocks, LANES), f32),
        in_specs=[SMEM] + [HBM] * 3,
        out_specs=VMEM,
        scratch_shapes=[
            *[pltpu.VMEM(a.shape, a.dtype) for a in (state, rates, mats)],
            pltpu.SemaphoreType.DMA((3,)),
            pltpu.VMEM((LANES, LANES), f32),
        ],
        compiler_params=pltpu.CompilerParams(vmem_limit_bytes=60 << 20),
    )(plan, state, rates, mats)


def local(
    n_gx, composition, particle_mass, mixing_rate, cell_index, section_counts,
    block_shuffle, batch_inverse, rate_exponents, stoichiometry,
):
    state, mats, plan = gather(
        n_gx, composition.transpose(1, 0, 2), particle_mass, mixing_rate, cell_index,
        section_counts[None], block_shuffle, batch_inverse.transpose(1, 0, 2), stoichiometry,
    )
    return react(plan, state, rate_exponents.T, mats).transpose(1, 0, 2)


def solution(mesh):
    both = ("gx", "yz")
    in_specs = (
        P(both, None, None), P(both, None), P(both, None), P(both, None), P(both),
        P(both, None), P(both, None, None), P(), P(),
    )
    return jax.shard_map(
        functools.partial(local, mesh.shape["gx"]),
        mesh=mesh, in_specs=in_specs, out_specs=P(both, None, None), check_vma=False,
    )
```

```python
import functools

import jax
import jax.numpy as jnp
from jax import lax
from jax.experimental import pallas as pl
from jax.experimental.pallas import tpu as pltpu
from jax.sharding import PartitionSpec as P

f32, bf16, f8 = jnp.float32, jnp.bfloat16, jnp.float8_e4m3fn
MESH = pl.DeviceIdType.MESH
VMEM = pl.BlockSpec(memory_space=pltpu.VMEM)
SMEM = pl.BlockSpec(memory_space=pltpu.SMEM)
HBM = pl.BlockSpec(memory_space=pltpu.HBM)

NS, NR, LANES = 20, 84, 128
CELL_DEV = 128
COLUMNS = 16
SLAB = CELL_DEV * COLUMNS
LOW = 256
HIGHS = 3 * SLAB // LOW
ROWS = 24
STEPS = 88
TILE = 16
GROUP = 32
STEP_SIZE = 0.25
PARTS = 64
TOP = 224.0
MASS_SCALE = 64.0
PACK = 4


def split(x):
    upper = x.astype(bf16)
    return upper, (x - upper.astype(f32)).astype(bf16)


def cut(x):
    first = x.astype(f8).astype(f32)
    second = (x - first).astype(f8).astype(f32)
    return first, second, x - first - second


def mm(a, b):
    return jnp.dot(a, b, preferred_element_type=f32)


def gather_kernel(
    n_gx, *refs,
):
    args, refs = refs[:8], refs[8:]
    outs = refs[:3]
    comp_ref, mass_ref, rate_ref, cell_ref, counts_ref, shuffle_ref, inverse_ref, stoich_ref = refs[3:11]
    (
        state_ref, mats_ref, plan_ref, fetch_sem, store_sem, square_ref,
        value_ref, low_ref, spread_ref, acc_ref, pick_ref, table_ref, wide_table_ref, part_ref, halo_ref, own_ref, sums_ref,
        mine_ref, near_ref, batch_ref, wide_ref, product_ref,
        halo_send, halo_recv, sum_send, sum_recv, mean_send, mean_recv, left_send, left_recv,
        right_send, right_recv, row_send, row_recv, batch_send, batch_recv,
    ) = refs[11:]
    fetches = [
        pltpu.make_async_copy(src, dst, fetch_sem.at[k])
        for k, (src, dst) in enumerate(zip(args, refs[3:11]))
    ]
    for copy in fetches:
        copy.start()
    blocks = mass_ref.shape[0]
    tiles = blocks // TILE
    i, j = lax.axis_index("gx"), lax.axis_index("yz")
    left, right = lax.rem(i + n_gx - 1, n_gx), lax.rem(i + 1, n_gx)
    first = (i - 1) * SLAB
    iota = lax.broadcasted_iota(jnp.int32, (LOW, LANES), 0).astype(f32).astype(bf16)
    one, zero = jnp.ones((), bf16), jnp.zeros((), bf16)
    own_highs = range(HIGHS // 3, 2 * HIGHS // 3)
    other_highs = [h for h in range(HIGHS) if h not in own_highs]

    def column(p):
        return lax.rem(j + p, COLUMNS)

    def gx_peer(p):
        return lax.rem(i + p, n_gx)

    def send(src, dst, send_sem, recv_sem, target):
        copy = pltpu.make_async_remote_copy(
            src_ref=src, dst_ref=dst, send_sem=send_sem, recv_sem=recv_sem,
            device_id=target, device_id_type=MESH,
        )
        copy.start()
        return copy

    barrier = pltpu.get_barrier_semaphore()
    peers = [(gx_peer(p), j) for p in range(1, n_gx)] + [(i, column(p)) for p in range(1, COLUMNS)]
    for target in peers:
        pl.semaphore_signal(barrier, inc=1, device_id=target, device_id_type=MESH)
    acc_ref[...] = jnp.zeros_like(acc_ref)
    square_ref[...] = jnp.zeros_like(square_ref)
    for copy in fetches:
        copy.wait()

    square_ref[:NS, :NS] = inverse_ref[:, 0, :]
    packed = square_ref[:PACK]
    for c in range(1, NS // PACK):
        packed = packed + pltpu.roll(square_ref[PACK * c : PACK * (c + 1)], c * ROWS, 1)
    batch_ref[j, i] = packed

    bound = jnp.max(jnp.abs(comp_ref[...]), keepdims=True).reshape(1, 1) * jnp.max(mass_ref[...], keepdims=True)
    bound = jnp.maximum(bound, 1e-30)
    scale, unscale = TOP / bound, bound / TOP

    def prepare(t):
        base = pl.multiple_of(t * TILE, TILE)
        low = ((cell_ref[pl.ds(base, TILE), :] - first) & (LOW - 1)).astype(f32)
        masses = mass_ref[pl.ds(base, TILE), :]
        for b in range(TILE):
            lanes = slice(b * LANES, (b + 1) * LANES)
            mass = masses[b : b + 1, :]
            value = cut(comp_ref[:, base + b, :] * (mass * scale))
            weight = cut(mass * MASS_SCALE)
            value_ref[t, :, lanes] = jnp.concatenate(
                [value[0], *weight, jnp.zeros((1, LANES), f32), value[1], value[2]], 0
            ).astype(bf16)
            low_row = jnp.broadcast_to(low[b : b + 1, :], (LOW, LANES)).astype(bf16)
            low_ref[t, :, lanes] = jnp.where(low_row == iota, one, zero).astype(f8)

    def spread(t, slot, highs):
        base = pl.multiple_of(t * TILE, TILE)
        high = ((cell_ref[pl.ds(base, TILE), :] - first) >> 8).astype(f32)
        for b in range(TILE):
            lanes = slice(b * LANES, (b + 1) * LANES)
            values = value_ref[t, :, lanes]
            high_row = jnp.broadcast_to(high[b : b + 1, :], (PARTS, LANES)).astype(bf16)
            for k, h in enumerate(highs):
                spread_ref[slot, k * PARTS : (k + 1) * PARTS, lanes] = jnp.where(
                    high_row == jnp.asarray(h, bf16), values, zero
                ).astype(f8)

    def accumulate(t, slot, highs):
        rows = len(highs) * PARTS
        acc_ref[:rows] += lax.dot_general(
            spread_ref[slot, :rows], low_ref[t], (((1,), (1,)), ((), ())), preferred_element_type=f32
        )

    def owners(highs):
        for k, h in enumerate(highs):
            sums = acc_ref[k * PARTS : (k + 1) * PARTS, :]
            value = (sums[:NS] + sums[ROWS : ROWS + NS] + sums[ROWS + NS :]) * unscale
            weight = (sums[NS : NS + 1] + sums[NS + 1 : NS + 2] + sums[NS + 2 : NS + 3]) * (1 / MASS_SCALE)
            total = jnp.concatenate([value, weight, jnp.zeros((ROWS - NS - 1, LOW), f32)], 0)
            yield k, total[:, :CELL_DEV], total[:, CELL_DEV:]


    def other_tiles(u, carry):
        for slot in range(2):
            prepare(2 * u + slot)
            spread(2 * u + slot, slot, other_highs)
            accumulate(2 * u + slot, slot, other_highs)
        return carry

    lax.fori_loop(0, tiles // 4, other_tiles, 0)
    pl.semaphore_wait(barrier, len(peers))
    rows = [
        send(batch_ref.at[j, i], batch_ref.at[j, i], row_send.at[p], row_recv.at[p], (gx_peer(p), j))
        for p in range(1, n_gx)
    ]
    lax.fori_loop(tiles // 4, tiles // 2, other_tiles, 0)
    for k, even, odd in owners(other_highs):
        part_ref[2 * k] = even
        part_ref[2 * k + 1] = odd
    acc_ref[...] = jnp.zeros_like(acc_ref)

    halos = [
        send(part_ref.at[pl.ds(0, COLUMNS)], halo_ref.at[1], halo_send.at[0], halo_recv.at[0], (left, j)),
        send(part_ref.at[pl.ds(COLUMNS, COLUMNS)], halo_ref.at[0], halo_send.at[1], halo_recv.at[1], (right, j)),
    ]
    for copy in rows:
        copy.wait()
    batches = [
        send(batch_ref.at[j], batch_ref.at[j], batch_send.at[p], batch_recv.at[p], (i, column(p)))
        for p in range(1, COLUMNS)
    ]

    def own_tiles(u, carry):
        for slot in range(2):
            spread(2 * u + slot, slot, own_highs)
            accumulate(2 * u + slot, slot, own_highs)
        return carry

    lax.fori_loop(0, tiles // 2, own_tiles, 0)

    row = lax.broadcasted_iota(jnp.int32, (blocks, blocks), 0)
    lane = lax.broadcasted_iota(jnp.int32, (blocks, blocks), 1)
    lane_f = lane.astype(f32)
    place = ((row % COLUMNS) * (blocks // COLUMNS) + row // COLUMNS).astype(f32)
    eye = row == lane
    counts = counts_ref[...].astype(f32)
    shuffle = shuffle_ref[...].astype(f32)
    block_of = jnp.sum(jnp.where(eye, shuffle, 0.0), axis=1, keepdims=True)
    count_of = jnp.sum(jnp.where(block_of == lane_f, counts, 0.0), axis=1, keepdims=True)
    count_row = jnp.sum(jnp.where(eye, count_of, 0.0), axis=0, keepdims=True)
    ahead = (count_row > count_of) | ((count_row == count_of) & (lane < row))
    rank = jnp.sum(jnp.where(ahead, 1.0, 0.0), axis=1, keepdims=True)
    here = rank == lane_f
    lines = [jnp.sum(jnp.where(here, v, 0.0), axis=0, keepdims=True) for v in (place, block_of, count_of)]
    plan_ref[...] = jnp.concatenate(lines + [jnp.zeros((5, blocks), f32)], 0).astype(jnp.int32)
    stores = [pltpu.make_async_copy(plan_ref, outs[2], store_sem.at[tiles // 2 + 1])]
    stores[0].start()

    for copy in halos:
        copy.wait()
    for k, even, odd in owners(own_highs):
        own_ref[2 * k] = even + halo_ref[0, 2 * k] + halo_ref[1, 2 * k]
        own_ref[2 * k + 1] = odd + halo_ref[0, 2 * k + 1] + halo_ref[1, 2 * k + 1]

    partials = [
        send(own_ref.at[column(p)], sums_ref.at[p], sum_send.at[p], sum_recv.at[p], (i, column(p)))
        for p in range(1, COLUMNS)
    ]

    wide_ref[...] = jnp.zeros_like(wide_ref)
    upper, lower = (v.astype(f32) for v in split(STEP_SIZE * stoich_ref[...]))
    for c in range(NS // PACK):
        for k, piece in enumerate((upper, lower, upper)):
            for start in (0, STEPS):
                lanes = slice(2 * c * LANES + start, 2 * c * LANES + start + NR)
                wide_ref[k * LANES + c * ROWS : k * LANES + c * ROWS + NS, lanes] = piece
    wide = wide_ref[...].astype(bf16)
    for copy in batches:
        copy.wait()
    batch_total = n_gx * COLUMNS
    for t in range(PACK):
        upper, lower = split(batch_ref[:, :, t, :].reshape(batch_total, LANES))
        product = mm(jnp.concatenate([upper, upper, lower], 1), wide)
        for c in range(NS // PACK):
            for side in range(2):
                at = (2 * c + side) * LANES
                product_ref[:, PACK * c + t, side * LANES : (side + 1) * LANES] = product[:, at : at + LANES]
    for r in range(NS, ROWS):
        product_ref[:, r, :] = jnp.zeros((batch_total, 2 * LANES), f32)
    total = own_ref[j]
    for p, copy in enumerate(partials, 1):
        copy.wait()
        total = total + sums_ref[p]
    means = total[:NS] / total[NS : NS + 1]
    mine_ref[...] = jnp.concatenate([means, jnp.zeros((ROWS - NS, CELL_DEV), f32)], 0)

    slab_means = [
        send(mine_ref, near_ref.at[COLUMNS + j], mean_send.at[p], mean_recv.at[p], (i, column(p)))
        for p in range(1, COLUMNS)
    ]
    near_ref[COLUMNS + j] = mine_ref[...]

    def forward(p, src, at):
        return [
            send(src, near_ref.at[2 * COLUMNS + at], left_send.at[p], left_recv.at[p], (left, j)),
            send(src, near_ref.at[at], right_send.at[p], right_recv.at[p], (right, j)),
        ]

    forwards = forward(0, mine_ref, j)

    once = lax.broadcasted_iota(jnp.int32, (ROWS, 2 * LANES), 1) < STEPS

    def pair(u, carry):
        for k in range(8):
            value = product_ref[8 * u + k]
            upper = value.astype(bf16).astype(f32)
            mats_ref[8 * u + k] = jnp.concatenate([upper, jnp.where(once, value - upper, 0.0)], 0).astype(bf16)
        return carry

    lax.fori_loop(0, batch_total // 8, pair, 0)
    stores.append(pltpu.make_async_copy(mats_ref, outs[1], store_sem.at[tiles // 2]))
    stores[1].start()

    for p, copy in enumerate(slab_means, 1):
        copy.wait()
        source = lax.rem(j - p + COLUMNS, COLUMNS)
        forwards += forward(p, near_ref.at[COLUMNS + source], source)

    def tabulate(highs):
        bound = jnp.zeros((ROWS, CELL_DEV), f32)
        for h in highs:
            bound = jnp.maximum(bound, jnp.maximum(jnp.abs(near_ref[2 * h]), jnp.abs(near_ref[2 * h + 1])))
        bound = jnp.maximum(jnp.max(bound, keepdims=True), 1e-30)
        for k, h in enumerate(highs):
            parts = cut(jnp.concatenate([near_ref[2 * h], near_ref[2 * h + 1]], 1) * (TOP / bound))
            for piece in range(3):
                wide_table_ref[piece, k * ROWS : (k + 1) * ROWS] = parts[piece]
        rows = len(highs) * ROWS
        table_ref[:, :rows] = wide_table_ref[:, :rows].astype(f8)
        return bound / TOP

    def pick(t, slot, highs):
        rows = len(highs) * ROWS
        pick_ref[slot, :rows] = sum(mm(table_ref[piece, :rows], low_ref[t]) for piece in range(3))

    def choose(t, slot, highs, b):
        base = pl.multiple_of(t * TILE, TILE)
        high = (cell_ref[pl.ds(base, TILE), :] - first) >> 8
        high_row = jnp.broadcast_to(high[b : b + 1, :], (ROWS, LANES))
        lanes = slice(b * LANES, (b + 1) * LANES)
        mean = jnp.zeros((ROWS, LANES), f32)
        for k, h in enumerate(highs):
            mean = jnp.where(high_row == h, pick_ref[slot, k * ROWS : (k + 1) * ROWS, lanes], mean)
        return mean

    own_unscale = tabulate(own_highs)

    def own_lookup(u, carry):
        for slot in range(2):
            t = 2 * u + slot
            pick(t, slot, own_highs)
            for b in range(TILE):
                state_ref[t * TILE + b] = choose(t, slot, own_highs, b) * own_unscale
        return carry

    lax.fori_loop(0, tiles // 2, own_lookup, 0)
    for copy in forwards:
        copy.wait()

    other_unscale = tabulate(other_highs)

    def other_lookup(u, carry):
        for slot in range(2):
            t = 2 * u + slot
            base = pl.multiple_of(t * TILE, TILE)
            pick(t, slot, other_highs)
            decay = jnp.exp(-rate_ref[pl.ds(base, TILE), :])
            for b in range(TILE):
                mean = (state_ref[base + b] + choose(t, slot, other_highs, b) * other_unscale)[:NS]
                state_ref[base + b, :NS] = mean + (comp_ref[:, base + b, :] - mean) * decay[b : b + 1, :]
                state_ref[base + b, NS:] = jnp.zeros((ROWS - NS, LANES), f32)
        store_state(u).start()
        return carry

    def store_state(u):
        part = pl.ds(pl.multiple_of(u * 2 * TILE, 2 * TILE), 2 * TILE)
        return pltpu.make_async_copy(state_ref.at[part], outs[0].at[part], store_sem.at[u])

    lax.fori_loop(0, tiles // 2, other_lookup, 0)
    for copy in stores:
        copy.wait()
    for u in range(tiles // 2):
        store_state(u).wait()


def gather(n_gx, *args):
    blocks = args[1].shape[0]
    dma = pltpu.SemaphoreType.DMA
    piece = (COLUMNS, ROWS, CELL_DEV)
    outs = (
        jax.ShapeDtypeStruct((blocks, ROWS, LANES), f32),
        jax.ShapeDtypeStruct((n_gx * COLUMNS, 2 * ROWS, 2 * LANES), bf16),
        jax.ShapeDtypeStruct((8, blocks), jnp.int32),
    )
    return pl.pallas_call(
        functools.partial(gather_kernel, n_gx),
        out_shape=outs,
        in_specs=[HBM] * 8,
        out_specs=(HBM,) * 3,
        scratch_shapes=[
            *[pltpu.VMEM(a.shape, a.dtype) for a in (*args, *outs)],
            dma((len(args),)),
            dma((blocks // TILE // 2 + 2,)),
            pltpu.VMEM((ROWS, LANES), f32),
            pltpu.VMEM((blocks // TILE, PARTS, TILE * LANES), bf16),
            pltpu.VMEM((blocks // TILE, LOW, TILE * LANES), f8),
            pltpu.VMEM((2, HIGHS * PARTS * 2 // 3, TILE * LANES), f8),
            pltpu.VMEM((HIGHS * PARTS * 2 // 3, LOW), f32),
            pltpu.VMEM((2, HIGHS * ROWS * 2 // 3, TILE * LANES), f32),
            pltpu.VMEM((3, HIGHS * ROWS * 2 // 3, LOW), f8),
            pltpu.VMEM((3, HIGHS * ROWS * 2 // 3, LOW), f32),
            pltpu.VMEM((2 * COLUMNS, ROWS, CELL_DEV), f32),
            pltpu.VMEM((2, *piece), f32),
            pltpu.VMEM(piece, f32),
            pltpu.VMEM(piece, f32),
            pltpu.VMEM((ROWS, CELL_DEV), f32),
            pltpu.VMEM((3 * COLUMNS, ROWS, CELL_DEV), f32),
            pltpu.VMEM((COLUMNS, n_gx, PACK, LANES), f32),
            pltpu.VMEM((3 * LANES, NS // PACK * 2 * LANES), f32),
            pltpu.VMEM((n_gx * COLUMNS, ROWS, 2 * LANES), f32),
            dma((2,)), dma((2,)), *[dma((COLUMNS,))] * 8,
            dma((n_gx,)), dma((n_gx,)), dma((COLUMNS,)), dma((COLUMNS,)),
        ],
        compiler_params=pltpu.CompilerParams(
            collective_id=0, has_side_effects=True, vmem_limit_bytes=60 << 20
        ),
    )(*args)


def react_kernel(plan_ref, *refs):
    args, (out_ref, state_ref, rates_ref, mats_ref, fetch_sem, turn_ref) = refs[:3], refs[3:]
    fetches = [
        pltpu.make_async_copy(src, dst, fetch_sem.at[k])
        for k, (src, dst) in enumerate(zip(args, (state_ref, rates_ref, mats_ref)))
    ]
    for copy in fetches:
        copy.start()
    blocks = state_ref.shape[0]
    turn_ref[...] = jnp.zeros_like(turn_ref)
    fetches[1].wait()
    upper, lower = (v.astype(f32) for v in split(rates_ref[...]))
    for k, piece in enumerate((upper, upper, lower)):
        turn_ref[k * ROWS : k * ROWS + NS, :NR] = piece
    rates = turn_ref[...].T[:STEPS, : 3 * ROWS].astype(bf16)
    fetches[0].wait()
    fetches[2].wait()

    def group(g, carry):
        at = [g * GROUP + b for b in range(GROUP)]
        batch, block, need = ([plan_ref[line, a] for a in at] for line in range(3))

        def section(s, states):
            x = jnp.concatenate(states, 1)
            upper = x.astype(bf16).astype(f32)
            progress = jnp.tanh(mm(rates, jnp.concatenate([upper, x - upper, upper], 0).astype(bf16)))
            upper = progress.astype(bf16).astype(f32)
            progress = jnp.concatenate([upper, progress - upper], 0).astype(bf16)
            products = [
                mm(
                    jnp.concatenate([mats_ref[batch[b]], mats_ref[batch[b + 1]]], 0)[:, : 2 * STEPS],
                    progress[:, b * LANES : (b + 2) * LANES],
                )
                for b in range(0, GROUP, 2)
            ]
            after = []
            for b, y in zip(range(0, GROUP, 2), products):
                for c in range(2):
                    mine = y[48 * c : 48 * c + 48, c * LANES : (c + 1) * LANES]
                    after.append(states[b + c] + jnp.where(s < need[b + c], mine[:24] + mine[24:], 0.0))
            return tuple(after)

        states = lax.fori_loop(0, need[0], section, tuple(state_ref[b] for b in block))
        for b in range(GROUP):
            out_ref[:, block[b], :] = states[b][:NS]
        return carry

    lax.fori_loop(0, blocks // GROUP, group, 0)


def react(plan, state, rates, mats):
    blocks = state.shape[0]
    return pl.pallas_call(
        react_kernel,
        out_shape=jax.ShapeDtypeStruct((NS, blocks, LANES), f32),
        in_specs=[SMEM] + [HBM] * 3,
        out_specs=VMEM,
        scratch_shapes=[
            *[pltpu.VMEM(a.shape, a.dtype) for a in (state, rates, mats)],
            pltpu.SemaphoreType.DMA((3,)),
            pltpu.VMEM((LANES, LANES), f32),
        ],
        compiler_params=pltpu.CompilerParams(vmem_limit_bytes=60 << 20),
    )(plan, state, rates, mats)


def local(
    n_gx, composition, particle_mass, mixing_rate, cell_index, section_counts,
    block_shuffle, batch_inverse, rate_exponents, stoichiometry,
):
    state, mats, plan = gather(
        n_gx, composition.transpose(1, 0, 2), particle_mass, mixing_rate, cell_index,
        section_counts[None], block_shuffle, batch_inverse.transpose(1, 0, 2), stoichiometry,
    )
    return react(plan, state, rate_exponents.T, mats).transpose(1, 0, 2)


def solution(mesh):
    both = ("gx", "yz")
    in_specs = (
        P(both, None, None), P(both, None), P(both, None), P(both, None), P(both),
        P(both, None), P(both, None, None), P(), P(),
    )
    return jax.shard_map(
        functools.partial(local, mesh.shape["gx"]),
        mesh=mesh, in_specs=in_specs, out_specs=P(both, None, None), check_vma=False,
    )
```

```python
import functools

import jax
import jax.numpy as jnp
from jax import lax
from jax.experimental import pallas as pl
from jax.experimental.pallas import tpu as pltpu
from jax.sharding import PartitionSpec as P

f32, bf16, f8 = jnp.float32, jnp.bfloat16, jnp.float8_e4m3fn
MESH = pl.DeviceIdType.MESH
VMEM = pl.BlockSpec(memory_space=pltpu.VMEM)
SMEM = pl.BlockSpec(memory_space=pltpu.SMEM)
HBM = pl.BlockSpec(memory_space=pltpu.HBM)

NS, NR, LANES = 20, 84, 128
CELL_DEV = 128
COLUMNS = 16
SLAB = CELL_DEV * COLUMNS
LOW = 256
HIGHS = 3 * SLAB // LOW
ROWS = 24
STEPS = 88
TILE = 16
GROUP = 32
STEP_SIZE = 0.25
PARTS = 64
TOP = 224.0
MASS_SCALE = 64.0
PACK = 4


def split(x):
    upper = x.astype(bf16)
    return upper, (x - upper.astype(f32)).astype(bf16)


def cut(x):
    first = x.astype(f8).astype(f32)
    second = (x - first).astype(f8).astype(f32)
    return first, second, x - first - second


def mm(a, b):
    return jnp.dot(a, b, preferred_element_type=f32)


def gather_kernel(
    n_gx, *refs,
):
    args, refs = refs[:8], refs[8:]
    outs = refs[:3]
    comp_ref, mass_ref, rate_ref, cell_ref, counts_ref, shuffle_ref, inverse_ref, stoich_ref = refs[3:11]
    (
        state_ref, mats_ref, plan_ref, fetch_sem, store_sem, square_ref,
        value_ref, low_ref, spread_ref, acc_ref, pick_ref, table_ref, wide_table_ref, part_ref, halo_ref, own_ref, sums_ref,
        mine_ref, near_ref, batch_ref, wide_ref, product_ref,
        halo_send, halo_recv, sum_send, sum_recv, mean_send, mean_recv, slab_send, slab_recv,
        row_send, row_recv, batch_send, batch_recv,
    ) = refs[11:]
    fetches = [
        pltpu.make_async_copy(src, dst, fetch_sem.at[k])
        for k, (src, dst) in enumerate(zip(args, refs[3:11]))
    ]
    for copy in fetches:
        copy.start()
    blocks = mass_ref.shape[0]
    tiles = blocks // TILE
    i, j = lax.axis_index("gx"), lax.axis_index("yz")
    left, right = lax.rem(i + n_gx - 1, n_gx), lax.rem(i + 1, n_gx)
    first = (i - 1) * SLAB
    iota = lax.broadcasted_iota(jnp.int32, (LOW, LANES), 0).astype(f32).astype(bf16)
    one, zero = jnp.ones((), bf16), jnp.zeros((), bf16)
    own_highs = range(HIGHS // 3, 2 * HIGHS // 3)
    other_highs = [h for h in range(HIGHS) if h not in own_highs]

    def column(p):
        return lax.rem(j + p, COLUMNS)

    def gx_peer(p):
        return lax.rem(i + p, n_gx)

    def send(src, dst, send_sem, recv_sem, target):
        copy = pltpu.make_async_remote_copy(
            src_ref=src, dst_ref=dst, send_sem=send_sem, recv_sem=recv_sem,
            device_id=target, device_id_type=MESH,
        )
        copy.start()
        return copy

    barrier = pltpu.get_barrier_semaphore()
    peers = [(gx_peer(p), j) for p in range(1, n_gx)] + [(i, column(p)) for p in range(1, COLUMNS)]
    for target in peers:
        pl.semaphore_signal(barrier, inc=1, device_id=target, device_id_type=MESH)
    acc_ref[...] = jnp.zeros_like(acc_ref)
    square_ref[...] = jnp.zeros_like(square_ref)
    for copy in fetches:
        copy.wait()

    square_ref[:NS, :NS] = inverse_ref[:, 0, :]
    packed = square_ref[:PACK]
    for c in range(1, NS // PACK):
        packed = packed + pltpu.roll(square_ref[PACK * c : PACK * (c + 1)], c * ROWS, 1)
    batch_ref[j, i] = packed

    bound = jnp.max(jnp.abs(comp_ref[...]), keepdims=True).reshape(1, 1) * jnp.max(mass_ref[...], keepdims=True)
    bound = jnp.maximum(bound, 1e-30)
    scale, unscale = TOP / bound, bound / TOP

    def prepare(t):
        base = pl.multiple_of(t * TILE, TILE)
        low = ((cell_ref[pl.ds(base, TILE), :] - first) & (LOW - 1)).astype(f32)
        masses = mass_ref[pl.ds(base, TILE), :]
        for b in range(TILE):
            lanes = slice(b * LANES, (b + 1) * LANES)
            mass = masses[b : b + 1, :]
            value = cut(comp_ref[:, base + b, :] * (mass * scale))
            weight = cut(mass * MASS_SCALE)
            value_ref[t, :, lanes] = jnp.concatenate(
                [value[0], *weight, jnp.zeros((1, LANES), f32), value[1], value[2]], 0
            ).astype(bf16)
            low_row = jnp.broadcast_to(low[b : b + 1, :], (LOW, LANES)).astype(bf16)
            low_ref[t, :, lanes] = jnp.where(low_row == iota, one, zero).astype(f8)

    def spread(t, slot, highs):
        base = pl.multiple_of(t * TILE, TILE)
        high = ((cell_ref[pl.ds(base, TILE), :] - first) >> 8).astype(f32)
        for b in range(TILE):
            lanes = slice(b * LANES, (b + 1) * LANES)
            values = value_ref[t, :, lanes]
            high_row = jnp.broadcast_to(high[b : b + 1, :], (PARTS, LANES)).astype(bf16)
            for k, h in enumerate(highs):
                spread_ref[slot, k * PARTS : (k + 1) * PARTS, lanes] = jnp.where(
                    high_row == jnp.asarray(h, bf16), values, zero
                ).astype(f8)

    def accumulate(t, slot, highs):
        rows = len(highs) * PARTS
        acc_ref[:rows] += lax.dot_general(
            spread_ref[slot, :rows], low_ref[t], (((1,), (1,)), ((), ())), preferred_element_type=f32
        )

    def owners(highs):
        for k, h in enumerate(highs):
            sums = acc_ref[k * PARTS : (k + 1) * PARTS, :]
            value = (sums[:NS] + sums[ROWS : ROWS + NS] + sums[ROWS + NS :]) * unscale
            weight = (sums[NS : NS + 1] + sums[NS + 1 : NS + 2] + sums[NS + 2 : NS + 3]) * (1 / MASS_SCALE)
            total = jnp.concatenate([value, weight, jnp.zeros((ROWS - NS - 1, LOW), f32)], 0)
            yield k, total[:, :CELL_DEV], total[:, CELL_DEV:]


    def other_tiles(u, carry):
        for slot in range(2):
            prepare(2 * u + slot)
            spread(2 * u + slot, slot, other_highs)
            accumulate(2 * u + slot, slot, other_highs)
        return carry

    lax.fori_loop(0, tiles // 4, other_tiles, 0)
    pl.semaphore_wait(barrier, len(peers))
    rows = [
        send(batch_ref.at[j, i], batch_ref.at[j, i], row_send.at[p], row_recv.at[p], (gx_peer(p), j))
        for p in range(1, n_gx)
    ]
    lax.fori_loop(tiles // 4, tiles // 2, other_tiles, 0)
    for k, even, odd in owners(other_highs):
        part_ref[2 * k] = even
        part_ref[2 * k + 1] = odd
    acc_ref[...] = jnp.zeros_like(acc_ref)

    halos = [
        send(part_ref.at[pl.ds(0, COLUMNS)], halo_ref.at[1], halo_send.at[0], halo_recv.at[0], (left, j)),
        send(part_ref.at[pl.ds(COLUMNS, COLUMNS)], halo_ref.at[0], halo_send.at[1], halo_recv.at[1], (right, j)),
    ]
    for copy in rows:
        copy.wait()
    batches = [
        send(batch_ref.at[j], batch_ref.at[j], batch_send.at[p], batch_recv.at[p], (i, column(p)))
        for p in range(1, COLUMNS)
    ]

    def own_tiles(u, carry):
        for slot in range(2):
            spread(2 * u + slot, slot, own_highs)
            accumulate(2 * u + slot, slot, own_highs)
        return carry

    lax.fori_loop(0, tiles // 2, own_tiles, 0)

    row = lax.broadcasted_iota(jnp.int32, (blocks, blocks), 0)
    lane = lax.broadcasted_iota(jnp.int32, (blocks, blocks), 1)
    lane_f = lane.astype(f32)
    place = ((row % COLUMNS) * (blocks // COLUMNS) + row // COLUMNS).astype(f32)
    eye = row == lane
    counts = counts_ref[...].astype(f32)
    shuffle = shuffle_ref[...].astype(f32)
    block_of = jnp.sum(jnp.where(eye, shuffle, 0.0), axis=1, keepdims=True)
    count_of = jnp.sum(jnp.where(block_of == lane_f, counts, 0.0), axis=1, keepdims=True)
    count_row = jnp.sum(jnp.where(eye, count_of, 0.0), axis=0, keepdims=True)
    ahead = (count_row > count_of) | ((count_row == count_of) & (lane < row))
    rank = jnp.sum(jnp.where(ahead, 1.0, 0.0), axis=1, keepdims=True)
    here = rank == lane_f
    lines = [jnp.sum(jnp.where(here, v, 0.0), axis=0, keepdims=True) for v in (place, block_of, count_of)]
    plan_ref[...] = jnp.concatenate(lines + [jnp.zeros((5, blocks), f32)], 0).astype(jnp.int32)
    stores = [pltpu.make_async_copy(plan_ref, outs[2], store_sem.at[tiles // 2 + 1])]
    stores[0].start()

    for copy in halos:
        copy.wait()
    for k, even, odd in owners(own_highs):
        own_ref[2 * k] = even + halo_ref[0, 2 * k] + halo_ref[1, 2 * k]
        own_ref[2 * k + 1] = odd + halo_ref[0, 2 * k + 1] + halo_ref[1, 2 * k + 1]

    partials = [
        send(own_ref.at[column(p)], sums_ref.at[p], sum_send.at[p], sum_recv.at[p], (i, column(p)))
        for p in range(1, COLUMNS)
    ]

    wide_ref[...] = jnp.zeros_like(wide_ref)
    upper, lower = (v.astype(f32) for v in split(STEP_SIZE * stoich_ref[...]))
    for c in range(NS // PACK):
        for k, piece in enumerate((upper, lower, upper)):
            for start in (0, STEPS):
                lanes = slice(2 * c * LANES + start, 2 * c * LANES + start + NR)
                wide_ref[k * LANES + c * ROWS : k * LANES + c * ROWS + NS, lanes] = piece
    wide = wide_ref[...].astype(bf16)
    for copy in batches:
        copy.wait()
    batch_total = n_gx * COLUMNS
    for t in range(PACK):
        upper, lower = split(batch_ref[:, :, t, :].reshape(batch_total, LANES))
        product = mm(jnp.concatenate([upper, upper, lower], 1), wide)
        for c in range(NS // PACK):
            for side in range(2):
                at = (2 * c + side) * LANES
                product_ref[:, PACK * c + t, side * LANES : (side + 1) * LANES] = product[:, at : at + LANES]
    for r in range(NS, ROWS):
        product_ref[:, r, :] = jnp.zeros((batch_total, 2 * LANES), f32)
    total = own_ref[j]
    for p, copy in enumerate(partials, 1):
        copy.wait()
        total = total + sums_ref[p]
    means = total[:NS] / total[NS : NS + 1]
    mine_ref[...] = jnp.concatenate([means, jnp.zeros((ROWS - NS, CELL_DEV), f32)], 0)

    slab_means = [
        send(mine_ref, near_ref.at[COLUMNS + j], mean_send.at[p], mean_recv.at[p], (i, column(p)))
        for p in range(1, COLUMNS)
    ]
    near_ref[COLUMNS + j] = mine_ref[...]

    once = lax.broadcasted_iota(jnp.int32, (ROWS, 2 * LANES), 1) < STEPS

    def pair(u, carry):
        for k in range(8):
            value = product_ref[8 * u + k]
            upper = value.astype(bf16).astype(f32)
            mats_ref[8 * u + k] = jnp.concatenate([upper, jnp.where(once, value - upper, 0.0)], 0).astype(bf16)
        return carry

    lax.fori_loop(0, batch_total // 8, pair, 0)
    stores.append(pltpu.make_async_copy(mats_ref, outs[1], store_sem.at[tiles // 2]))
    stores[1].start()

    for copy in slab_means:
        copy.wait()
    own = near_ref.at[pl.ds(COLUMNS, COLUMNS)]
    forwards = [
        send(own, near_ref.at[pl.ds(2 * COLUMNS, COLUMNS)], slab_send.at[0], slab_recv.at[0], (left, j)),
        send(own, near_ref.at[pl.ds(0, COLUMNS)], slab_send.at[1], slab_recv.at[1], (right, j)),
    ]

    def tabulate(highs):
        bound = jnp.zeros((ROWS, CELL_DEV), f32)
        for h in highs:
            bound = jnp.maximum(bound, jnp.maximum(jnp.abs(near_ref[2 * h]), jnp.abs(near_ref[2 * h + 1])))
        bound = jnp.maximum(jnp.max(bound, keepdims=True), 1e-30)
        for k, h in enumerate(highs):
            parts = cut(jnp.concatenate([near_ref[2 * h], near_ref[2 * h + 1]], 1) * (TOP / bound))
            for piece in range(3):
                wide_table_ref[piece, k * ROWS : (k + 1) * ROWS] = parts[piece]
        rows = len(highs) * ROWS
        table_ref[:, :rows] = wide_table_ref[:, :rows].astype(f8)
        return bound / TOP

    def pick(t, slot, highs):
        rows = len(highs) * ROWS
        pick_ref[slot, :rows] = sum(mm(table_ref[piece, :rows], low_ref[t]) for piece in range(3))

    def choose(t, slot, highs, b):
        base = pl.multiple_of(t * TILE, TILE)
        high = (cell_ref[pl.ds(base, TILE), :] - first) >> 8
        high_row = jnp.broadcast_to(high[b : b + 1, :], (ROWS, LANES))
        lanes = slice(b * LANES, (b + 1) * LANES)
        mean = jnp.zeros((ROWS, LANES), f32)
        for k, h in enumerate(highs):
            mean = jnp.where(high_row == h, pick_ref[slot, k * ROWS : (k + 1) * ROWS, lanes], mean)
        return mean

    own_unscale = tabulate(own_highs)

    def own_lookup(u, carry):
        for slot in range(2):
            t = 2 * u + slot
            pick(t, slot, own_highs)
            for b in range(TILE):
                state_ref[t * TILE + b] = choose(t, slot, own_highs, b) * own_unscale
        return carry

    lax.fori_loop(0, tiles // 2, own_lookup, 0)
    for copy in forwards:
        copy.wait()

    other_unscale = tabulate(other_highs)

    def other_lookup(u, carry):
        for slot in range(2):
            t = 2 * u + slot
            base = pl.multiple_of(t * TILE, TILE)
            pick(t, slot, other_highs)
            decay = jnp.exp(-rate_ref[pl.ds(base, TILE), :])
            for b in range(TILE):
                mean = (state_ref[base + b] + choose(t, slot, other_highs, b) * other_unscale)[:NS]
                state_ref[base + b, :NS] = mean + (comp_ref[:, base + b, :] - mean) * decay[b : b + 1, :]
                state_ref[base + b, NS:] = jnp.zeros((ROWS - NS, LANES), f32)
        store_state(u).start()
        return carry

    def store_state(u):
        part = pl.ds(pl.multiple_of(u * 2 * TILE, 2 * TILE), 2 * TILE)
        return pltpu.make_async_copy(state_ref.at[part], outs[0].at[part], store_sem.at[u])

    lax.fori_loop(0, tiles // 2, other_lookup, 0)
    for copy in stores:
        copy.wait()
    for u in range(tiles // 2):
        store_state(u).wait()


def gather(n_gx, *args):
    blocks = args[1].shape[0]
    dma = pltpu.SemaphoreType.DMA
    piece = (COLUMNS, ROWS, CELL_DEV)
    outs = (
        jax.ShapeDtypeStruct((blocks, ROWS, LANES), f32),
        jax.ShapeDtypeStruct((n_gx * COLUMNS, 2 * ROWS, 2 * LANES), bf16),
        jax.ShapeDtypeStruct((8, blocks), jnp.int32),
    )
    return pl.pallas_call(
        functools.partial(gather_kernel, n_gx),
        out_shape=outs,
        in_specs=[HBM] * 8,
        out_specs=(HBM,) * 3,
        scratch_shapes=[
            *[pltpu.VMEM(a.shape, a.dtype) for a in (*args, *outs)],
            dma((len(args),)),
            dma((blocks // TILE // 2 + 2,)),
            pltpu.VMEM((ROWS, LANES), f32),
            pltpu.VMEM((blocks // TILE, PARTS, TILE * LANES), bf16),
            pltpu.VMEM((blocks // TILE, LOW, TILE * LANES), f8),
            pltpu.VMEM((2, HIGHS * PARTS * 2 // 3, TILE * LANES), f8),
            pltpu.VMEM((HIGHS * PARTS * 2 // 3, LOW), f32),
            pltpu.VMEM((2, HIGHS * ROWS * 2 // 3, TILE * LANES), f32),
            pltpu.VMEM((3, HIGHS * ROWS * 2 // 3, LOW), f8),
            pltpu.VMEM((3, HIGHS * ROWS * 2 // 3, LOW), f32),
            pltpu.VMEM((2 * COLUMNS, ROWS, CELL_DEV), f32),
            pltpu.VMEM((2, *piece), f32),
            pltpu.VMEM(piece, f32),
            pltpu.VMEM(piece, f32),
            pltpu.VMEM((ROWS, CELL_DEV), f32),
            pltpu.VMEM((3 * COLUMNS, ROWS, CELL_DEV), f32),
            pltpu.VMEM((COLUMNS, n_gx, PACK, LANES), f32),
            pltpu.VMEM((3 * LANES, NS // PACK * 2 * LANES), f32),
            pltpu.VMEM((n_gx * COLUMNS, ROWS, 2 * LANES), f32),
            dma((2,)), dma((2,)), *[dma((COLUMNS,))] * 4, dma((2,)), dma((2,)),
            dma((n_gx,)), dma((n_gx,)), dma((COLUMNS,)), dma((COLUMNS,)),
        ],
        compiler_params=pltpu.CompilerParams(
            collective_id=0, has_side_effects=True, vmem_limit_bytes=60 << 20
        ),
    )(*args)


def react_kernel(plan_ref, *refs):
    args, (out_ref, state_ref, rates_ref, mats_ref, fetch_sem, turn_ref) = refs[:3], refs[3:]
    fetches = [
        pltpu.make_async_copy(src, dst, fetch_sem.at[k])
        for k, (src, dst) in enumerate(zip(args, (state_ref, rates_ref, mats_ref)))
    ]
    for copy in fetches:
        copy.start()
    blocks = state_ref.shape[0]
    turn_ref[...] = jnp.zeros_like(turn_ref)
    fetches[1].wait()
    upper, lower = (v.astype(f32) for v in split(rates_ref[...]))
    for k, piece in enumerate((upper, upper, lower)):
        turn_ref[k * ROWS : k * ROWS + NS, :NR] = piece
    rates = turn_ref[...].T[:STEPS, : 3 * ROWS].astype(bf16)
    fetches[0].wait()
    fetches[2].wait()

    def group(g, carry):
        at = [g * GROUP + b for b in range(GROUP)]
        batch, block, need = ([plan_ref[line, a] for a in at] for line in range(3))

        def section(s, states):
            x = jnp.concatenate(states, 1)
            upper = x.astype(bf16).astype(f32)
            progress = jnp.tanh(mm(rates, jnp.concatenate([upper, x - upper, upper], 0).astype(bf16)))
            upper = progress.astype(bf16).astype(f32)
            progress = jnp.concatenate([upper, progress - upper], 0).astype(bf16)
            products = [
                mm(
                    jnp.concatenate([mats_ref[batch[b]], mats_ref[batch[b + 1]]], 0)[:, : 2 * STEPS],
                    progress[:, b * LANES : (b + 2) * LANES],
                )
                for b in range(0, GROUP, 2)
            ]
            after = []
            for b, y in zip(range(0, GROUP, 2), products):
                for c in range(2):
                    mine = y[48 * c : 48 * c + 48, c * LANES : (c + 1) * LANES]
                    after.append(states[b + c] + jnp.where(s < need[b + c], mine[:24] + mine[24:], 0.0))
            return tuple(after)

        states = lax.fori_loop(0, need[0], section, tuple(state_ref[b] for b in block))
        for b in range(GROUP):
            out_ref[:, block[b], :] = states[b][:NS]
        return carry

    lax.fori_loop(0, blocks // GROUP, group, 0)


def react(plan, state, rates, mats):
    blocks = state.shape[0]
    return pl.pallas_call(
        react_kernel,
        out_shape=jax.ShapeDtypeStruct((NS, blocks, LANES), f32),
        in_specs=[SMEM] + [HBM] * 3,
        out_specs=VMEM,
        scratch_shapes=[
            *[pltpu.VMEM(a.shape, a.dtype) for a in (state, rates, mats)],
            pltpu.SemaphoreType.DMA((3,)),
            pltpu.VMEM((LANES, LANES), f32),
        ],
        compiler_params=pltpu.CompilerParams(vmem_limit_bytes=60 << 20),
    )(plan, state, rates, mats)


def local(
    n_gx, composition, particle_mass, mixing_rate, cell_index, section_counts,
    block_shuffle, batch_inverse, rate_exponents, stoichiometry,
):
    state, mats, plan = gather(
        n_gx, composition.transpose(1, 0, 2), particle_mass, mixing_rate, cell_index,
        section_counts[None], block_shuffle, batch_inverse.transpose(1, 0, 2), stoichiometry,
    )
    return react(plan, state, rate_exponents.T, mats).transpose(1, 0, 2)


def solution(mesh):
    both = ("gx", "yz")
    in_specs = (
        P(both, None, None), P(both, None), P(both, None), P(both, None), P(both),
        P(both, None), P(both, None, None), P(), P(),
    )
    return jax.shard_map(
        functools.partial(local, mesh.shape["gx"]),
        mesh=mesh, in_specs=in_specs, out_specs=P(both, None, None), check_vma=False,
    )
```

```python
import functools

import jax
import jax.numpy as jnp
from jax import lax
from jax.experimental import pallas as pl
from jax.experimental.pallas import tpu as pltpu
from jax.sharding import PartitionSpec as P

f32, bf16, f8 = jnp.float32, jnp.bfloat16, jnp.float8_e4m3fn
MESH = pl.DeviceIdType.MESH
VMEM = pl.BlockSpec(memory_space=pltpu.VMEM)
SMEM = pl.BlockSpec(memory_space=pltpu.SMEM)
HBM = pl.BlockSpec(memory_space=pltpu.HBM)

NS, NR, LANES = 20, 84, 128
CELL_DEV = 128
COLUMNS = 16
SLAB = CELL_DEV * COLUMNS
LOW = 256
HIGHS = 3 * SLAB // LOW
ROWS = 24
STEPS = 88
TILE = 8
GROUP = 32
STEP_SIZE = 0.25
PARTS = 64
TOP = 224.0
MASS_SCALE = 64.0
PACK = 4


def split(x):
    upper = x.astype(bf16)
    return upper, (x - upper.astype(f32)).astype(bf16)


def cut(x):
    first = x.astype(f8).astype(f32)
    second = (x - first).astype(f8).astype(f32)
    return first, second, x - first - second


def mm(a, b):
    return jnp.dot(a, b, preferred_element_type=f32)


def gather_kernel(
    n_gx, *refs,
):
    args, refs = refs[:8], refs[8:]
    outs = refs[:3]
    comp_ref, mass_ref, rate_ref, cell_ref, counts_ref, shuffle_ref, inverse_ref, stoich_ref = refs[3:11]
    (
        state_ref, mats_ref, plan_ref, fetch_sem, store_sem, square_ref,
        value_ref, low_ref, spread_ref, acc_ref, pick_ref, table_ref, wide_table_ref, part_ref, halo_ref, own_ref, sums_ref,
        mine_ref, near_ref, batch_ref, wide_ref, product_ref,
        halo_send, halo_recv, sum_send, sum_recv, mean_send, mean_recv, slab_send, slab_recv,
        row_send, row_recv, batch_send, batch_recv,
    ) = refs[11:]
    fetches = [
        pltpu.make_async_copy(src, dst, fetch_sem.at[k])
        for k, (src, dst) in enumerate(zip(args, refs[3:11]))
    ]
    for copy in fetches:
        copy.start()
    blocks = mass_ref.shape[0]
    tiles = blocks // TILE
    i, j = lax.axis_index("gx"), lax.axis_index("yz")
    left, right = lax.rem(i + n_gx - 1, n_gx), lax.rem(i + 1, n_gx)
    first = (i - 1) * SLAB
    iota = lax.broadcasted_iota(jnp.int32, (LOW, LANES), 0).astype(f32).astype(bf16)
    one, zero = jnp.ones((), bf16), jnp.zeros((), bf16)
    own_highs = range(HIGHS // 3, 2 * HIGHS // 3)
    other_highs = [h for h in range(HIGHS) if h not in own_highs]

    def column(p):
        return lax.rem(j + p, COLUMNS)

    def gx_peer(p):
        return lax.rem(i + p, n_gx)

    def send(src, dst, send_sem, recv_sem, target):
        copy = pltpu.make_async_remote_copy(
            src_ref=src, dst_ref=dst, send_sem=send_sem, recv_sem=recv_sem,
            device_id=target, device_id_type=MESH,
        )
        copy.start()
        return copy

    barrier = pltpu.get_barrier_semaphore()
    peers = [(gx_peer(p), j) for p in range(1, n_gx)] + [(i, column(p)) for p in range(1, COLUMNS)]
    for target in peers:
        pl.semaphore_signal(barrier, inc=1, device_id=target, device_id_type=MESH)
    acc_ref[...] = jnp.zeros_like(acc_ref)
    square_ref[...] = jnp.zeros_like(square_ref)
    for copy in fetches:
        copy.wait()

    square_ref[:NS, :NS] = inverse_ref[:, 0, :]
    packed = square_ref[:PACK]
    for c in range(1, NS // PACK):
        packed = packed + pltpu.roll(square_ref[PACK * c : PACK * (c + 1)], c * ROWS, 1)
    batch_ref[j, i] = packed

    bound = jnp.max(jnp.abs(comp_ref[...]), keepdims=True).reshape(1, 1) * jnp.max(mass_ref[...], keepdims=True)
    bound = jnp.maximum(bound, 1e-30)
    scale, unscale = TOP / bound, bound / TOP

    def prepare(t):
        base = pl.multiple_of(t * TILE, TILE)
        low = ((cell_ref[pl.ds(base, TILE), :] - first) & (LOW - 1)).astype(f32)
        masses = mass_ref[pl.ds(base, TILE), :]
        for b in range(TILE):
            lanes = slice(b * LANES, (b + 1) * LANES)
            mass = masses[b : b + 1, :]
            value = cut(comp_ref[:, base + b, :] * (mass * scale))
            weight = cut(mass * MASS_SCALE)
            value_ref[t, :, lanes] = jnp.concatenate(
                [value[0], *weight, jnp.zeros((1, LANES), f32), value[1], value[2]], 0
            ).astype(bf16)
            low_row = jnp.broadcast_to(low[b : b + 1, :], (LOW, LANES)).astype(bf16)
            low_ref[t, :, lanes] = jnp.where(low_row == iota, one, zero).astype(f8)

    def spread(t, slot, highs):
        base = pl.multiple_of(t * TILE, TILE)
        high = ((cell_ref[pl.ds(base, TILE), :] - first) >> 8).astype(f32)
        for b in range(TILE):
            lanes = slice(b * LANES, (b + 1) * LANES)
            values = value_ref[t, :, lanes]
            high_row = jnp.broadcast_to(high[b : b + 1, :], (PARTS, LANES)).astype(bf16)
            for k, h in enumerate(highs):
                spread_ref[slot, k * PARTS : (k + 1) * PARTS, lanes] = jnp.where(
                    high_row == jnp.asarray(h, bf16), values, zero
                ).astype(f8)

    def accumulate(t, slot, highs):
        rows = len(highs) * PARTS
        acc_ref[:rows] += lax.dot_general(
            spread_ref[slot, :rows], low_ref[t], (((1,), (1,)), ((), ())), preferred_element_type=f32
        )

    def owners(highs):
        for k, h in enumerate(highs):
            sums = acc_ref[k * PARTS : (k + 1) * PARTS, :]
            value = (sums[:NS] + sums[ROWS : ROWS + NS] + sums[ROWS + NS :]) * unscale
            weight = (sums[NS : NS + 1] + sums[NS + 1 : NS + 2] + sums[NS + 2 : NS + 3]) * (1 / MASS_SCALE)
            total = jnp.concatenate([value, weight, jnp.zeros((ROWS - NS - 1, LOW), f32)], 0)
            yield k, total[:, :CELL_DEV], total[:, CELL_DEV:]


    def other_tiles(u, carry):
        for slot in range(2):
            prepare(2 * u + slot)
            spread(2 * u + slot, slot, other_highs)
            accumulate(2 * u + slot, slot, other_highs)
        return carry

    lax.fori_loop(0, tiles // 4, other_tiles, 0)
    pl.semaphore_wait(barrier, len(peers))
    rows = [
        send(batch_ref.at[j, i], batch_ref.at[j, i], row_send.at[p], row_recv.at[p], (gx_peer(p), j))
        for p in range(1, n_gx)
    ]
    lax.fori_loop(tiles // 4, tiles // 2, other_tiles, 0)
    for k, even, odd in owners(other_highs):
        part_ref[2 * k] = even
        part_ref[2 * k + 1] = odd
    acc_ref[...] = jnp.zeros_like(acc_ref)

    halos = [
        send(part_ref.at[pl.ds(0, COLUMNS)], halo_ref.at[1], halo_send.at[0], halo_recv.at[0], (left, j)),
        send(part_ref.at[pl.ds(COLUMNS, COLUMNS)], halo_ref.at[0], halo_send.at[1], halo_recv.at[1], (right, j)),
    ]
    for copy in rows:
        copy.wait_recv()
    batches = [
        send(batch_ref.at[j], batch_ref.at[j], batch_send.at[p], batch_recv.at[p], (i, column(p)))
        for p in range(1, COLUMNS)
    ]

    def own_tiles(u, carry):
        for slot in range(2):
            spread(2 * u + slot, slot, own_highs)
            accumulate(2 * u + slot, slot, own_highs)
        return carry

    lax.fori_loop(0, tiles // 2, own_tiles, 0)

    row = lax.broadcasted_iota(jnp.int32, (blocks, blocks), 0)
    lane = lax.broadcasted_iota(jnp.int32, (blocks, blocks), 1)
    lane_f = lane.astype(f32)
    place = ((row % COLUMNS) * (blocks // COLUMNS) + row // COLUMNS).astype(f32)
    eye = row == lane
    counts = counts_ref[...].astype(f32)
    shuffle = shuffle_ref[...].astype(f32)
    block_of = jnp.sum(jnp.where(eye, shuffle, 0.0), axis=1, keepdims=True)
    count_of = jnp.sum(jnp.where(block_of == lane_f, counts, 0.0), axis=1, keepdims=True)
    count_row = jnp.sum(jnp.where(eye, count_of, 0.0), axis=0, keepdims=True)
    ahead = (count_row > count_of) | ((count_row == count_of) & (lane < row))
    rank = jnp.sum(jnp.where(ahead, 1.0, 0.0), axis=1, keepdims=True)
    here = rank == lane_f
    lines = [jnp.sum(jnp.where(here, v, 0.0), axis=0, keepdims=True) for v in (place, block_of, count_of)]
    plan_ref[...] = jnp.concatenate(lines + [jnp.zeros((5, blocks), f32)], 0).astype(jnp.int32)
    stores = [pltpu.make_async_copy(plan_ref, outs[2], store_sem.at[tiles // 2 + 1])]
    stores[0].start()

    for copy in halos:
        copy.wait_recv()
    for k, even, odd in owners(own_highs):
        own_ref[2 * k] = even + halo_ref[0, 2 * k] + halo_ref[1, 2 * k]
        own_ref[2 * k + 1] = odd + halo_ref[0, 2 * k + 1] + halo_ref[1, 2 * k + 1]

    partials = [
        send(own_ref.at[column(p)], sums_ref.at[p], sum_send.at[p], sum_recv.at[p], (i, column(p)))
        for p in range(1, COLUMNS)
    ]

    wide_ref[...] = jnp.zeros_like(wide_ref)
    upper, lower = (v.astype(f32) for v in split(STEP_SIZE * stoich_ref[...]))
    for c in range(NS // PACK):
        for k, piece in enumerate((upper, lower, upper)):
            for start in (0, STEPS):
                lanes = slice(2 * c * LANES + start, 2 * c * LANES + start + NR)
                wide_ref[k * LANES + c * ROWS : k * LANES + c * ROWS + NS, lanes] = piece
    wide = wide_ref[...].astype(bf16)
    for copy in batches:
        copy.wait_recv()
    batch_total = n_gx * COLUMNS
    for t in range(PACK):
        upper, lower = split(batch_ref[:, :, t, :].reshape(batch_total, LANES))
        product = mm(jnp.concatenate([upper, upper, lower], 1), wide)
        for c in range(NS // PACK):
            for side in range(2):
                at = (2 * c + side) * LANES
                product_ref[:, PACK * c + t, side * LANES : (side + 1) * LANES] = product[:, at : at + LANES]
    for r in range(NS, ROWS):
        product_ref[:, r, :] = jnp.zeros((batch_total, 2 * LANES), f32)
    total = own_ref[j]
    for p, copy in enumerate(partials, 1):
        copy.wait_recv()
        total = total + sums_ref[p]
    means = total[:NS] / total[NS : NS + 1]
    mine_ref[...] = jnp.concatenate([means, jnp.zeros((ROWS - NS, CELL_DEV), f32)], 0)

    slab_means = [
        send(mine_ref, near_ref.at[COLUMNS + j], mean_send.at[p], mean_recv.at[p], (i, column(p)))
        for p in range(1, COLUMNS)
    ]
    near_ref[COLUMNS + j] = mine_ref[...]

    once = lax.broadcasted_iota(jnp.int32, (ROWS, 2 * LANES), 1) < STEPS

    def pair(u, carry):
        for k in range(8):
            value = product_ref[8 * u + k]
            upper = value.astype(bf16).astype(f32)
            mats_ref[8 * u + k] = jnp.concatenate([upper, jnp.where(once, value - upper, 0.0)], 0).astype(bf16)
        return carry

    lax.fori_loop(0, batch_total // 8, pair, 0)
    stores.append(pltpu.make_async_copy(mats_ref, outs[1], store_sem.at[tiles // 2]))
    stores[1].start()

    for copy in slab_means:
        copy.wait_recv()
    own = near_ref.at[pl.ds(COLUMNS, COLUMNS)]
    forwards = [
        send(own, near_ref.at[pl.ds(2 * COLUMNS, COLUMNS)], slab_send.at[0], slab_recv.at[0], (left, j)),
        send(own, near_ref.at[pl.ds(0, COLUMNS)], slab_send.at[1], slab_recv.at[1], (right, j)),
    ]

    def tabulate(highs):
        bound = jnp.zeros((ROWS, CELL_DEV), f32)
        for h in highs:
            bound = jnp.maximum(bound, jnp.maximum(jnp.abs(near_ref[2 * h]), jnp.abs(near_ref[2 * h + 1])))
        bound = jnp.maximum(jnp.max(bound, keepdims=True), 1e-30)
        for k, h in enumerate(highs):
            parts = cut(jnp.concatenate([near_ref[2 * h], near_ref[2 * h + 1]], 1) * (TOP / bound))
            for piece in range(3):
                wide_table_ref[piece, k * ROWS : (k + 1) * ROWS] = parts[piece]
        rows = len(highs) * ROWS
        table_ref[:, :rows] = wide_table_ref[:, :rows].astype(f8)
        return bound / TOP

    def pick(t, slot, highs):
        rows = len(highs) * ROWS
        pick_ref[slot, :rows] = sum(mm(table_ref[piece, :rows], low_ref[t]) for piece in range(3))

    def choose(t, slot, highs, b):
        base = pl.multiple_of(t * TILE, TILE)
        high = (cell_ref[pl.ds(base, TILE), :] - first) >> 8
        high_row = jnp.broadcast_to(high[b : b + 1, :], (ROWS, LANES))
        lanes = slice(b * LANES, (b + 1) * LANES)
        mean = jnp.zeros((ROWS, LANES), f32)
        for k, h in enumerate(highs):
            mean = jnp.where(high_row == h, pick_ref[slot, k * ROWS : (k + 1) * ROWS, lanes], mean)
        return mean

    own_unscale = tabulate(own_highs)

    def own_lookup(u, carry):
        for slot in range(2):
            t = 2 * u + slot
            pick(t, slot, own_highs)
            for b in range(TILE):
                state_ref[t * TILE + b] = choose(t, slot, own_highs, b) * own_unscale
        return carry

    lax.fori_loop(0, tiles // 2, own_lookup, 0)
    for copy in forwards:
        copy.wait_recv()

    other_unscale = tabulate(other_highs)

    def other_lookup(u, carry):
        for slot in range(2):
            t = 2 * u + slot
            base = pl.multiple_of(t * TILE, TILE)
            pick(t, slot, other_highs)
            decay = jnp.exp(-rate_ref[pl.ds(base, TILE), :])
            for b in range(TILE):
                mean = (state_ref[base + b] + choose(t, slot, other_highs, b) * other_unscale)[:NS]
                state_ref[base + b, :NS] = mean + (comp_ref[:, base + b, :] - mean) * decay[b : b + 1, :]
                state_ref[base + b, NS:] = jnp.zeros((ROWS - NS, LANES), f32)
        store_state(u).start()
        return carry

    def store_state(u):
        part = pl.ds(pl.multiple_of(u * 2 * TILE, 2 * TILE), 2 * TILE)
        return pltpu.make_async_copy(state_ref.at[part], outs[0].at[part], store_sem.at[u])

    lax.fori_loop(0, tiles // 2, other_lookup, 0)
    for copy in stores:
        copy.wait()
    for copy in rows + halos + batches + partials + slab_means + forwards:
        copy.wait_send()
    for u in range(tiles // 2):
        store_state(u).wait()


def gather(n_gx, *args):
    blocks = args[1].shape[0]
    dma = pltpu.SemaphoreType.DMA
    piece = (COLUMNS, ROWS, CELL_DEV)
    outs = (
        jax.ShapeDtypeStruct((blocks, ROWS, LANES), f32),
        jax.ShapeDtypeStruct((n_gx * COLUMNS, 2 * ROWS, 2 * LANES), bf16),
        jax.ShapeDtypeStruct((8, blocks), jnp.int32),
    )
    return pl.pallas_call(
        functools.partial(gather_kernel, n_gx),
        out_shape=outs,
        in_specs=[HBM] * 8,
        out_specs=(HBM,) * 3,
        scratch_shapes=[
            *[pltpu.VMEM(a.shape, a.dtype) for a in (*args, *outs)],
            dma((len(args),)),
            dma((blocks // TILE // 2 + 2,)),
            pltpu.VMEM((ROWS, LANES), f32),
            pltpu.VMEM((blocks // TILE, PARTS, TILE * LANES), bf16),
            pltpu.VMEM((blocks // TILE, LOW, TILE * LANES), f8),
            pltpu.VMEM((2, HIGHS * PARTS * 2 // 3, TILE * LANES), f8),
            pltpu.VMEM((HIGHS * PARTS * 2 // 3, LOW), f32),
            pltpu.VMEM((2, HIGHS * ROWS * 2 // 3, TILE * LANES), f32),
            pltpu.VMEM((3, HIGHS * ROWS * 2 // 3, LOW), f8),
            pltpu.VMEM((3, HIGHS * ROWS * 2 // 3, LOW), f32),
            pltpu.VMEM((2 * COLUMNS, ROWS, CELL_DEV), f32),
            pltpu.VMEM((2, *piece), f32),
            pltpu.VMEM(piece, f32),
            pltpu.VMEM(piece, f32),
            pltpu.VMEM((ROWS, CELL_DEV), f32),
            pltpu.VMEM((3 * COLUMNS, ROWS, CELL_DEV), f32),
            pltpu.VMEM((COLUMNS, n_gx, PACK, LANES), f32),
            pltpu.VMEM((3 * LANES, NS // PACK * 2 * LANES), f32),
            pltpu.VMEM((n_gx * COLUMNS, ROWS, 2 * LANES), f32),
            dma((2,)), dma((2,)), *[dma((COLUMNS,))] * 4, dma((2,)), dma((2,)),
            dma((n_gx,)), dma((n_gx,)), dma((COLUMNS,)), dma((COLUMNS,)),
        ],
        compiler_params=pltpu.CompilerParams(
            collective_id=0, has_side_effects=True, vmem_limit_bytes=60 << 20
        ),
    )(*args)


def react_kernel(plan_ref, *refs):
    args, (out_ref, state_ref, rates_ref, mats_ref, fetch_sem, turn_ref) = refs[:3], refs[3:]
    fetches = [
        pltpu.make_async_copy(src, dst, fetch_sem.at[k])
        for k, (src, dst) in enumerate(zip(args, (state_ref, rates_ref, mats_ref)))
    ]
    for copy in fetches:
        copy.start()
    blocks = state_ref.shape[0]
    turn_ref[...] = jnp.zeros_like(turn_ref)
    fetches[1].wait()
    upper, lower = (v.astype(f32) for v in split(rates_ref[...]))
    for k, piece in enumerate((upper, upper, lower)):
        turn_ref[k * ROWS : k * ROWS + NS, :NR] = piece
    rates = turn_ref[...].T[:STEPS, : 3 * ROWS].astype(bf16)
    fetches[0].wait()
    fetches[2].wait()

    def group(g, carry):
        at = [g * GROUP + b for b in range(GROUP)]
        batch, block, need = ([plan_ref[line, a] for a in at] for line in range(3))

        def section(s, states):
            x = jnp.concatenate(states, 1)
            upper = x.astype(bf16).astype(f32)
            progress = jnp.tanh(mm(rates, jnp.concatenate([upper, x - upper, upper], 0).astype(bf16)))
            upper = progress.astype(bf16).astype(f32)
            progress = jnp.concatenate([upper, progress - upper], 0).astype(bf16)
            products = [
                mm(
                    jnp.concatenate([mats_ref[batch[b]], mats_ref[batch[b + 1]]], 0)[:, : 2 * STEPS],
                    progress[:, b * LANES : (b + 2) * LANES],
                )
                for b in range(0, GROUP, 2)
            ]
            after = []
            for b, y in zip(range(0, GROUP, 2), products):
                for c in range(2):
                    mine = y[48 * c : 48 * c + 48, c * LANES : (c + 1) * LANES]
                    after.append(states[b + c] + jnp.where(s < need[b + c], mine[:24] + mine[24:], 0.0))
            return tuple(after)

        states = lax.fori_loop(0, need[0], section, tuple(state_ref[b] for b in block))
        for b in range(GROUP):
            out_ref[:, block[b], :] = states[b][:NS]
        return carry

    lax.fori_loop(0, blocks // GROUP, group, 0)


def react(plan, state, rates, mats):
    blocks = state.shape[0]
    return pl.pallas_call(
        react_kernel,
        out_shape=jax.ShapeDtypeStruct((NS, blocks, LANES), f32),
        in_specs=[SMEM] + [HBM] * 3,
        out_specs=VMEM,
        scratch_shapes=[
            *[pltpu.VMEM(a.shape, a.dtype) for a in (state, rates, mats)],
            pltpu.SemaphoreType.DMA((3,)),
            pltpu.VMEM((LANES, LANES), f32),
        ],
        compiler_params=pltpu.CompilerParams(vmem_limit_bytes=60 << 20),
    )(plan, state, rates, mats)


def local(
    n_gx, composition, particle_mass, mixing_rate, cell_index, section_counts,
    block_shuffle, batch_inverse, rate_exponents, stoichiometry,
):
    state, mats, plan = gather(
        n_gx, composition.transpose(1, 0, 2), particle_mass, mixing_rate, cell_index,
        section_counts[None], block_shuffle, batch_inverse.transpose(1, 0, 2), stoichiometry,
    )
    return react(plan, state, rate_exponents.T, mats).transpose(1, 0, 2)


def solution(mesh):
    both = ("gx", "yz")
    in_specs = (
        P(both, None, None), P(both, None), P(both, None), P(both, None), P(both),
        P(both, None), P(both, None, None), P(), P(),
    )
    return jax.shard_map(
        functools.partial(local, mesh.shape["gx"]),
        mesh=mesh, in_specs=in_specs, out_specs=P(both, None, None), check_vma=False,
    )
```
